32 devices in a mesh: groups: 2 (over y), domain: 4 (over z), shot: 4 (over x, core).
Axes of the slice: x: 2, y: 2, z: 4, core: 2. Of those that a mesh axis runs over, the one named last changes fastest.
Arguments:
- velocity: float32 [16, 384, 128], P(('groups', 'domain'), 'shot'), parts along dimension 0, may hold values from 0.04 to 0.12
- thomsen_eps: float32 [16, 384, 128], P(('groups', 'domain'), 'shot'), parts along dimension 0, may hold values from 0.1 to 0.4
- thomsen_delta: float32 [16, 384, 128], P(('groups', 'domain'), 'shot'), parts along dimension 0, may hold values from 0 to 0.2
- tilt_angle: float32 [16, 384, 128], P(('groups', 'domain'), 'shot'), parts along dimension 0, may hold values from -1.2 to 1.2
- azimuth: float32 [16, 384, 128], P(('groups', 'domain'), 'shot'), parts along dimension 0, may hold values from -3.140625 to 3.140625
- shot_anchor: int32 [8], P(('groups', 'shot')), parts along dimension 0, may hold values from 0 to 192
- source_x: int32 [8], P(('groups', 'shot')), parts along dimension 0, may hold values from 0 to 7
- source_y: int32 [8], P(('groups', 'shot')), parts along dimension 0, may hold values from 0 to 191
- wavelet: float32 [8, 8], P(('groups', 'shot')), parts along dimension 0, may hold values from -64 to 64
- receiver_x: int32 [8, 256], P(('groups', 'shot')), parts along dimension 0, may hold values from 0 to 7
- receiver_y: int32 [8, 256], P(('groups', 'shot')), parts along dimension 0, may hold values from 0 to 191
- traces: float32 [8, 8, 256], P(('groups', 'shot')), parts along dimension 0, may hold values from -48 to 48
- source_now: float32 [8, 2, 8, 192, 128], P(('groups', 'shot'), None, 'domain'), parts along dimension 0, may hold values from -6 to 6
- source_before: float32 [8, 2, 8, 192, 128], P(('groups', 'shot'), None, 'domain'), parts along dimension 0, may hold values from -6 to 6
- receiver_now: float32 [8, 2, 8, 192, 128], P(('groups', 'shot'), None, 'domain'), parts along dimension 0, may hold values from -6 to 6
- receiver_before: float32 [8, 2, 8, 192, 128], P(('groups', 'shot'), None, 'domain'), parts along dimension 0, may hold values from -6 to 6
- slab_owner: int32 [8], P('groups'), parts along dimension 0, may hold values from 0 to 3, each once
Outputs:
- image: float32 [16, 384, 128], P(('groups', 'domain'), 'shot'), parts along dimension 0
The draws below stay inside these ranges and needn't reach their ends.
There are 2 independent parts, one for each index of `groups`. The reference program is written for one: setup_inputs(seed, part) draws one part's arguments, and reference() takes and returns one part's arrays. A program takes and returns all parts, laid end to end along the dimension named above; each array names one. Nothing has to cross between parts.
Inputs may be any that keep to these rules, and one draw needn't show every extreme that they name: `receiver_y`: receivers may share a cell. `slab_owner`: each slab index appears once.
All inputs are finite; a program needn't handle non-finite values.
Results may differ from the reference program's by a relative error of at most 0.0003.
Values sent between devices are 32-bit elements; how exact they have to be, the bound alone decides.
No kernel may reach another device: no remote copies, remote signals or barrier semaphores. Data moves between devices by JAX's collectives and lax.ppermute only.
A program may use at most 64 MiB of HBM per device.

```python
import math
import jax
import jax.numpy as jnp
from jax import lax

NY = 192
NZ = 128
NREC = 256
STEPS = 8
SRC_Z = 3
REC_Z = 1
AX = 8
IY = 384
SHOTS = 4


def with_ends(entries, own_key, least, top_value):
    longest = entries.shape.index(max(entries.shape))
    spots = []
    for shift in (0, 1):
        where = [jax.random.randint(jax.random.fold_in(own_key, axis), (), 0, length) for axis, length in enumerate(entries.shape)]
        where[longest] = (where[longest] + shift) % entries.shape[longest]
        spots.append(tuple(where))
    return entries.at[spots[0]].set(least).at[spots[1]].set(top_value)


def level_of(stream_key, dims, split, smallest, high):
    gain, own = 1.0, jax.random.fold_in(stream_key, 6)
    for position, shards_of in split:
        steps = jnp.exp(jax.random.uniform(jax.random.fold_in(own, position), (shards_of,), jnp.float32, smallest / len(split), high / len(split)))
        gain = gain * jnp.repeat(steps, dims[position] // shards_of).reshape([-1 if axis == position else 1 for axis in range(len(dims))])
    return gain


def centred(key, dims, scale, bound, cuts=(), dtype=jnp.bfloat16):
    factor_of = level_of(key, dims, cuts, -0.22, 0.18) if cuts else 1.0
    drawn = jax.random.normal(key, dims, jnp.float32) * scale * factor_of
    return jnp.minimum(jnp.maximum(drawn, -bound), bound).astype(dtype)


def setup_inputs(seed: int = 0, part: int = 0) -> dict:
    key_of = jax.random.split(jax.random.key(seed), 18)
    own_keys = jax.random.split(jax.random.fold_in(key_of[17], part), 18)
    velocity = jnp.clip(jnp.exp(math.log(0.12) - 1.0986123 * jax.random.uniform(own_keys[0], (AX, IY, NZ), jnp.float32) ** level_of(own_keys[0], (AX, IY, NZ), ((0, 4), (1, 4)), -0.2, 0.2)), 0.04, 0.12)
    thomsen_eps = jnp.clip(0.1 + 0.3 * jax.random.uniform(own_keys[1], (AX, IY, NZ), jnp.float32) ** level_of(own_keys[1], (AX, IY, NZ), ((0, 4), (1, 4)), -0.2, 0.2), 0.1, 0.4)
    thomsen_delta = jnp.clip(0.2 * jax.random.uniform(own_keys[2], (AX, IY, NZ), jnp.float32) ** level_of(own_keys[2], (AX, IY, NZ), ((0, 4), (1, 4)), -0.2, 0.2), 0.0, 0.2)
    tilt_angle = jnp.clip(jax.random.uniform(own_keys[3], (AX, IY, NZ), jnp.float32, -1.2, 1.2) * level_of(own_keys[3], (AX, IY, NZ), ((0, 4), (1, 4)), -0.4, 0.0), -1.2, 1.2)
    azimuth = jnp.clip(jax.random.uniform(own_keys[4], (AX, IY, NZ), jnp.float32, -3.140625, 3.140625), -3.140625, 3.140625)
    shot_anchor = with_ends(jax.random.randint(own_keys[5], (SHOTS,), 0, NY + 1), jax.random.fold_in(own_keys[5], 1), 0, NY).astype(jnp.int32)
    source_x = with_ends(jax.random.randint(own_keys[6], (SHOTS,), 0, AX), jax.random.fold_in(own_keys[6], 1), 0, AX - 1).astype(jnp.int32)
    source_y = with_ends(jax.random.randint(own_keys[7], (SHOTS,), 0, NY), jax.random.fold_in(own_keys[7], 1), 0, NY - 1).astype(jnp.int32)
    wavelet = centred(own_keys[8], (SHOTS, STEPS), 16.0, 64.0, ((0, 4),), jnp.float32)
    receiver_x = with_ends(jax.random.randint(own_keys[9], (SHOTS, NREC), 0, AX), jax.random.fold_in(own_keys[9], 1), 0, AX - 1).astype(jnp.int32)
    receiver_y = with_ends(jax.random.randint(own_keys[10], (SHOTS, NREC), 0, NY), jax.random.fold_in(own_keys[10], 1), 0, NY - 1).astype(jnp.int32)
    traces = centred(own_keys[11], (SHOTS, STEPS, NREC), 8.0, 48.0, ((0, 4),), jnp.float32)
    source_now = centred(own_keys[12], (SHOTS, 2, AX, NY, NZ), 1.0, 6.0, ((0, 4), (2, 4)), jnp.float32)
    source_before = centred(own_keys[13], (SHOTS, 2, AX, NY, NZ), 1.0, 6.0, ((0, 4), (2, 4)), jnp.float32)
    receiver_now = centred(own_keys[14], (SHOTS, 2, AX, NY, NZ), 1.0, 6.0, ((0, 4), (2, 4)), jnp.float32)
    receiver_before = centred(own_keys[15], (SHOTS, 2, AX, NY, NZ), 1.0, 6.0, ((0, 4), (2, 4)), jnp.float32)
    slab_owner = jax.random.permutation(own_keys[16], SHOTS).astype(jnp.int32)
    return {"velocity": velocity, "thomsen_eps": thomsen_eps, "thomsen_delta": thomsen_delta, "tilt_angle": tilt_angle, "azimuth": azimuth, "shot_anchor": shot_anchor, "source_x": source_x, "source_y": source_y, "wavelet": wavelet, "receiver_x": receiver_x, "receiver_y": receiver_y, "traces": traces, "source_now": source_now, "source_before": source_before, "receiver_now": receiver_now, "receiver_before": receiver_before, "slab_owner": slab_owner}


def coefficients(velocity, thomsen_eps, thomsen_delta, tilt_angle, azimuth):
    gain_eps = 1.0 + 2.0 * thomsen_eps
    gain_delta = jnp.sqrt(1.0 + 2.0 * thomsen_delta)
    axis_x = jnp.sin(tilt_angle) * jnp.cos(azimuth)
    axis_y = jnp.sin(tilt_angle) * jnp.sin(azimuth)
    axis_z = jnp.cos(tilt_angle)
    return (velocity, gain_eps, gain_delta, axis_x, axis_y, axis_z)

def second_derivs(padded):
    middle = padded[1:-1, 1:-1, 1:-1]
    second_xx = padded[2:, 1:-1, 1:-1] - 2.0 * middle + padded[:-2, 1:-1, 1:-1]
    second_yy = padded[1:-1, 2:, 1:-1] - 2.0 * middle + padded[1:-1, :-2, 1:-1]
    second_zz = padded[1:-1, 1:-1, 2:] - 2.0 * middle + padded[1:-1, 1:-1, :-2]
    mixed_xy = 0.25 * (padded[2:, 2:, 1:-1] - padded[2:, :-2, 1:-1] - padded[:-2, 2:, 1:-1] + padded[:-2, :-2, 1:-1])
    mixed_xz = 0.25 * (padded[2:, 1:-1, 2:] - padded[2:, 1:-1, :-2] - padded[:-2, 1:-1, 2:] + padded[:-2, 1:-1, :-2])
    mixed_yz = 0.25 * (padded[1:-1, 2:, 2:] - padded[1:-1, 2:, :-2] - padded[1:-1, :-2, 2:] + padded[1:-1, :-2, :-2])
    return (second_xx, second_yy, second_zz, mixed_xy, mixed_xz, mixed_yz)

def along_axis(derivs, axis_x, axis_y, axis_z):
    second_xx, second_yy, second_zz, mixed_xy, mixed_xz, mixed_yz = derivs
    pure = axis_x * axis_x * second_xx + axis_y * axis_y * second_yy + axis_z * axis_z * second_zz
    return pure + 2.0 * (axis_x * axis_y * mixed_xy + axis_x * axis_z * mixed_xz + axis_y * axis_z * mixed_yz)

def wave_update(padded, previous, local_coefs):
    courant, gain_eps, gain_delta, axis_x, axis_y, axis_z = local_coefs
    results = []
    for field in (0, 2):
        derivs_p = second_derivs(padded[field])
        derivs_q = second_derivs(padded[field + 1])
        axial_p = along_axis(derivs_p, axis_x, axis_y, axis_z)
        across_p = derivs_p[0] + derivs_p[1] + derivs_p[2] - axial_p
        axial_q = along_axis(derivs_q, axis_x, axis_y, axis_z)
        cur_p = padded[field][1:-1, 1:-1, 1:-1]
        cur_q = padded[field + 1][1:-1, 1:-1, 1:-1]
        new_p = 2.0 * cur_p - previous[field] + courant * (gain_eps * across_p + gain_delta * axial_q)
        new_q = 2.0 * cur_q - previous[field + 1] + courant * (gain_delta * across_p + axial_q)
        results.append(new_p)
        results.append(new_q)
    return jnp.stack(results)

def inject(updated, courant, source_plane, receiver_plane):
    updated = updated.at[0:2, :, :, SRC_Z].add(courant[None, :, :, SRC_Z] * source_plane[None])
    updated = updated.at[2:4, :, :, REC_Z].add(courant[None, :, :, REC_Z] * receiver_plane[None])
    return updated

def reference(velocity, thomsen_eps, thomsen_delta, tilt_angle, azimuth, shot_anchor, source_x, source_y, wavelet, receiver_x, receiver_y, traces, source_now, source_before, receiver_now, receiver_before, slab_owner):
    x_ids = jnp.arange(AX).astype(jnp.int32)
    lane_ids = jnp.arange(NY).astype(jnp.int32)

    def per_shot(total, shot_data):
        anchor, src_x, src_y, wave_row, rec_x, rec_y, trace_rows, src_now, src_before, rec_now, rec_before = shot_data
        pieces = [lax.dynamic_slice_in_dim(field, anchor, NY, 1) for field in (velocity, thomsen_eps, thomsen_delta, tilt_angle, azimuth)]
        local_coefs = coefficients(pieces[0], pieces[1], pieces[2], pieces[3], pieces[4])
        source_plane = ((x_ids[:, None] == src_x) & (lane_ids[None, :] == src_y)).astype(jnp.float32)

        def one_step(step_id, states):
            current, previous, image_sum = states
            padded = jnp.pad(current, ((0, 0), (1, 1), (1, 1), (1, 1)))
            updated = wave_update(padded, previous, local_coefs)
            receiver_plane = jnp.zeros((AX, NY), jnp.float32).at[rec_x, rec_y].add(trace_rows[step_id])
            updated = inject(updated, local_coefs[0], source_plane * wave_row[step_id], receiver_plane)
            return (updated, current, image_sum + updated[0] * updated[2])
        current = jnp.concatenate([src_now, rec_now], axis=0)
        previous = jnp.concatenate([src_before, rec_before], axis=0)
        start_image = jnp.zeros((AX, NY, NZ), jnp.float32)
        final = lax.fori_loop(0, STEPS, one_step, (current, previous, start_image))
        placed = lax.dynamic_update_slice(jnp.zeros((AX, IY, NZ), jnp.float32), final[2], (jnp.int32(0), anchor.astype(jnp.int32), jnp.int32(0)))
        return (total + placed, None)
    start_total = jnp.zeros((AX, IY, NZ), jnp.float32)
    total, unused = lax.scan(per_shot, start_total, (shot_anchor, source_x, source_y, wavelet, receiver_x, receiver_y, traces, source_now, source_before, receiver_now, receiver_before))
    blocks = total.reshape(AX, SHOTS, IY // SHOTS, NZ)
    image = jnp.take(blocks, slab_owner, axis=1).reshape(AX, IY, NZ) / STEPS
    return image
```

```python
import functools

import jax
import jax.numpy as jnp
from jax import lax
from jax.experimental import pallas as pl
from jax.experimental.pallas import tpu as pltpu
from jax.sharding import PartitionSpec as P

SRC_Z = 3
REC_Z = 1
TILE = 8
COEFS = 16
LIMIT = 40 * 1024 * 1024


class Layout:
    def __init__(self, domain, shots, rows, lines, steps):
        self.domain, self.shots, self.rows, self.lines, self.steps = domain, shots, rows, lines, steps
        self.half = domain // 2
        self.part = rows // 2
        self.width = rows * domain
        self.own = lines // domain
        halo = -(-steps // TILE) * TILE
        if self.half == 2 and self.own % TILE == 0:
            self.pad = (0, 0)
            self.chip = 2 * self.own + halo
            self.stride = lines - self.chip
            self.span = self.own + 2 * halo
        else:
            self.chip = -(-(2 * self.own + 2 * halo) // TILE) * TILE
            self.pad = (halo, max(0, (self.half - 1) * 2 * self.own + self.chip - halo - lines))
            self.stride = 2 * self.own
            self.span = self.chip

    def start(self, kc):
        return kc * self.stride

    def shift(self, c):
        return c * (self.chip - self.span)

    def rounds(self):
        count = self.domain * self.shots
        for r in range(self.domain):
            pairs = []
            for d in range(self.domain):
                for s in range(self.shots):
                    k = (d + r) % self.domain
                    to_d = self.half * (s & 1) + (k >> 1)
                    to_s = (s & ~1) | (k & 1)
                    pairs.append((d * self.shots + s, to_d * self.shots + to_s))
            assert len({pair[1] for pair in pairs}) == count
            yield r, pairs


def swapped(value, axis, bit):
    count = lax.axis_size(axis)
    return lax.ppermute(value, axis, [(i, i ^ bit) for i in range(count)])


def gather_rows(info_ref, lay, own_refs, other_refs, store):
    kc, c = info_ref[0], info_ref[1]
    shift = pl.multiple_of(info_ref[2], TILE)
    for core, refs in ((c, own_refs), (1 - c, other_refs)):
        k = 2 * kc + core
        for r, ref in enumerate(refs):
            source = lax.rem(k - r + lay.domain, lay.domain)
            for part in range(lay.part):
                store(source * lay.rows + core * lay.part + part, part, ref, shift)


def make_coefs(raw_ref, coef_ref, lay):
    lane = lax.broadcasted_iota(jnp.int32, (lay.span, raw_ref.shape[-1]), 1)
    last = raw_ref.shape[-1] - 1

    def from_below(value):
        return jnp.where(lane == 0, 0.0, pltpu.roll(value, 1, 1))

    def from_above(value):
        return jnp.where(lane == last, 0.0, pltpu.roll(value, last, 1))

    def one_row(row, unused):
        velocity, eps, delta, tilt, azimuth = (raw_ref[i, row] for i in range(5))
        gain_eps = 1.0 + 2.0 * eps
        gain_delta = jnp.sqrt(1.0 + 2.0 * delta)
        sin_tilt = jnp.sin(tilt)
        n_x = sin_tilt * jnp.cos(azimuth)
        n_y = sin_tilt * jnp.sin(azimuth)
        n_z = jnp.cos(tilt)
        xx, yy, zz = n_x * n_x, n_y * n_y, n_z * n_z
        xz, yz = 0.5 * n_x * n_z, 0.5 * n_y * n_z
        values = (
            xx, 1.0 - xx, yy, 1.0 - yy, 0.5 * n_x * n_y,
            from_below(zz), from_below(1.0 - zz), from_below(xz), from_below(yz),
            from_above(zz), from_above(1.0 - zz), from_above(xz), from_above(yz),
            velocity * gain_eps, velocity * gain_delta, velocity,
        )
        for i, value in enumerate(values):
            coef_ref[i, row] = value
        return unused

    lax.fori_loop(0, lay.width, one_row, 0)


def run_steps(state, coef_ref, inject_ref, depth, lay, after):
    z_count = state.shape[-1]
    last = z_count - 1
    lane = lax.broadcasted_iota(jnp.int32, (TILE, z_count), 1)
    chunk = next(size for size in (8, 4, 2, 1) if lay.width % size == 0)

    def row_of(now, field, row, tile):
        base = TILE + TILE * tile
        middle = state[now, field, row, base : base + TILE, :]
        low = state[now, field, row, base - 1 : base - 1 + TILE, :]
        high = state[now, field, row, base + 1 : base + 1 + TILE, :]
        return middle, high - low, high + low

    def one_step(step, unused):
        now = lax.rem(step, 2)
        new = 1 - now
        turn = lax.rem(depth - step + z_count, z_count)

        def one_chunk(first):
            for tile in range(lay.span // TILE):
                lines = slice(TILE * tile, TILE * tile + TILE)
                inner = slice(TILE + TILE * tile, 2 * TILE + TILE * tile)
                before = [row_of(now, field, first, tile) for field in (0, 1)]
                here = [row_of(now, field, first + 1, tile) for field in (0, 1)]
                for i in range(chunk):
                    row = first + i
                    beyond = [row_of(now, field, row + 2, tile) for field in (0, 1)]
                    coef = [coef_ref[n, row, lines, :] for n in range(COEFS)]
                    xx, xx0, yy, yy0, xy = coef[:5]
                    zz_b, zz0_b, xz_b, yz_b, zz_a, zz0_a, xz_a, yz_a = coef[5:13]
                    axial_gain, cross_gain, velocity = coef[13:]

                    def terms(field):
                        f, diff_y, sum_y = here[field]
                        sum_x = beyond[field][0] + before[field][0]
                        diff_x = beyond[field][0] - before[field][0]
                        mixed = beyond[field][1] - before[field][1]
                        below = xz_b * diff_x + yz_b * diff_y
                        above = xz_a * diff_x + yz_a * diff_y
                        return f, sum_x, sum_y, xy * mixed, below, above

                    p, sum_x, sum_y, mixed, below, above = terms(0)
                    across = xx0 * sum_x + yy0 * sum_y - mixed
                    across += pltpu.roll(zz0_b * p - below, last, 1) + pltpu.roll(zz0_a * p + above, 1, 1)
                    across -= 4.0 * p
                    q, sum_x, sum_y, mixed, below, above = terms(1)
                    axial = xx * sum_x + yy * sum_y + mixed
                    axial += pltpu.roll(zz_b * q + below, last, 1) + pltpu.roll(zz_a * q - above, 1, 1)
                    axial -= 2.0 * q
                    pulse = pltpu.roll(inject_ref[row, lines, :], turn, 1)
                    pulse = velocity * jnp.where(lane == depth, pulse, 0.0)
                    old_p = state[new, 0, row + 1, inner, :]
                    old_q = state[new, 1, row + 1, inner, :]
                    new_p = (p + p - old_p) + (axial_gain * across + cross_gain * axial) + pulse
                    new_q = (q + q - old_q) + (cross_gain * across + velocity * axial) + pulse
                    state[new, 0, row + 1, inner, :] = new_p
                    state[new, 1, row + 1, inner, :] = new_q
                    after(step, row, lines, new_p)
                    before, here = here, beyond

        if chunk == lay.width:
            one_chunk(0)
        else:
            lax.fori_loop(0, lay.width // chunk, lambda n, u: (one_chunk(n * chunk), u)[1], 0)
        return unused

    lax.fori_loop(0, lay.steps, one_step, 0)


def clear_edges(state, lay):
    rows, lines = state.shape[2], state.shape[3]
    edge = jnp.zeros((lines,) + state.shape[4:], jnp.float32)
    strip = jnp.zeros((rows, TILE) + state.shape[4:], jnp.float32)
    for time in (0, 1):
        for field in (0, 1):
            state[time, field, 0] = edge
            state[time, field, rows - 1] = edge
            state[time, field, :, :TILE] = strip
            state[time, field, :, lines - TILE :] = strip


def source_kernel(lay, info_ref, inject_ref, *refs):
    count = lay.domain
    waves_own, waves_other, model_own, model_other = (refs[i * count : (i + 1) * count] for i in range(4))
    coef_ref, history_ref, raw, state = refs[4 * count :]
    clear_edges(state, lay)

    def store_wave(row, part, ref, shift):
        for time in (0, 1):
            for field in (0, 1):
                state[time, field, row + 1, TILE : TILE + lay.span, :] = ref[
                    2 * time + field, part, pl.ds(shift, lay.span), :
                ]

    def store_model(row, part, ref, shift):
        for i in range(5):
            raw[i, row] = ref[i, part, pl.ds(shift, lay.span), :]

    gather_rows(info_ref, lay, waves_own, waves_other, store_wave)
    gather_rows(info_ref, lay, model_own, model_other, store_model)
    make_coefs(raw, coef_ref, lay)

    def after(step, row, lines, new_p):
        history_ref[step, row, lines, :] = new_p

    run_steps(state, coef_ref, inject_ref, SRC_Z, lay, after)


def receiver_kernel(lay, info_ref, inject_ref, coef_ref, history_ref, *refs):
    count = lay.domain
    waves_own, waves_other, old_own, old_other = (refs[i * count : (i + 1) * count] for i in range(4))
    image_ref, state = refs[4 * count :]
    clear_edges(state, lay)

    def store_now(row, part, ref, shift):
        for field in (0, 1):
            state[0, field, row + 1, TILE : TILE + lay.span, :] = ref[4 + field, part, pl.ds(shift, lay.span), :]

    def store_old(row, part, ref, shift):
        for field in (0, 1):
            state[1, field, row + 1, TILE : TILE + lay.span, :] = ref[field, part, pl.ds(shift, lay.span), :]

    gather_rows(info_ref, lay, waves_own, waves_other, store_now)
    gather_rows(info_ref, lay, old_own, old_other, store_old)
    image_ref[...] = jnp.zeros_like(image_ref)

    def after(step, row, lines, new_p):
        image_ref[row, lines, :] += history_ref[step, row, lines, :] * new_p

    run_steps(state, coef_ref, inject_ref, REC_Z, lay, after)


def call(kernel, lay, outs, scratch, info, *operands):
    vmem = pl.BlockSpec(memory_space=pltpu.VMEM)
    return pl.pallas_call(
        functools.partial(kernel, lay),
        out_shape=outs,
        in_specs=[pl.BlockSpec(memory_space=pltpu.SMEM)] + [vmem] * len(operands),
        out_specs=jax.tree.map(lambda unused: vmem, outs),
        scratch_shapes=scratch,
        compiler_params=pltpu.CompilerParams(vmem_limit_bytes=LIMIT),
    )(info, *operands)


def per_device(
    velocity,
    thomsen_eps,
    thomsen_delta,
    tilt_angle,
    azimuth,
    shot_anchor,
    source_x,
    source_y,
    wavelet,
    receiver_x,
    receiver_y,
    traces,
    source_now,
    source_before,
    receiver_now,
    receiver_before,
    slab_owner,
):
    rows, lines, z_count = source_now.shape[2:]
    steps = wavelet.shape[1]
    domain, shots = lax.axis_size("domain"), lax.axis_size("shot")
    lay = Layout(domain, shots, rows, lines, steps)
    d, s = lax.axis_index("domain"), lax.axis_index("shot")
    core = s & 1
    chip_id = lax.rem(d, lay.half)
    works_on = d // lay.half
    zero = jnp.int32(0)

    def send(pick):
        own, other = [], []
        for r, pairs in lay.rounds():
            k = lax.rem(d + r, domain)
            message = lax.ppermute(pick(k & 1, k >> 1), ("domain", "shot"), pairs)
            own.append(message)
            other.append(swapped(message, "shot", 1))
        return own + other

    def wave_pick(*fields):
        fields = [jnp.pad(field[0], ((0, 0), (0, 0), lay.pad, (0, 0))) for field in fields]

        def pick(c, kc):
            return jnp.concatenate(
                [
                    lax.dynamic_slice(
                        field,
                        (zero, c * lay.part, lay.start(kc), zero),
                        (2, lay.part, lay.chip, z_count),
                    )
                    for field in fields
                ]
            )

        return pick

    waves = send(wave_pick(source_now, source_before, receiver_now))

    model = jnp.stack([velocity, thomsen_eps, thomsen_delta, tilt_angle, azimuth])
    slab = model.shape[2]
    model = model[:, :, None]
    bit = shots // 2
    while bit:
        twin = swapped(model, "shot", bit)
        upper = (s & bit) != 0
        model = jnp.stack([jnp.where(upper, twin, model), jnp.where(upper, model, twin)], axis=3)
        model = model.reshape(model.shape[:2] + (-1,) + model.shape[4:])
        bit //= 2
    model = model.reshape(model.shape[:2] + (shots * slab, z_count))
    anchor = shot_anchor[0]
    if lay.pad != (0, 0):
        model = lax.dynamic_slice_in_dim(model, anchor, lines, 2)
        model = jnp.pad(model, ((0, 0), (0, 0), lay.pad, (0, 0)))
        first_line = zero
    else:
        first_line = anchor

    def model_pick(c, kc):
        return lax.dynamic_slice(
            model,
            (zero, c * lay.part, first_line + lay.start(kc), zero),
            (5, lay.part, lay.chip, z_count),
        )

    models = send(model_pick)
    olds = send(wave_pick(receiver_before))

    receivers = receiver_x.shape[1]
    mine = jnp.concatenate(
        [
            traces[0].reshape(-1),
            wavelet[0],
            receiver_x[0].astype(jnp.float32),
            receiver_y[0].astype(jnp.float32),
            source_x.astype(jnp.float32),
            source_y.astype(jnp.float32),
            shot_anchor.astype(jnp.float32),
        ]
    )
    twin = swapped(mine, "shot", 1)
    table = jnp.where(works_on == core, mine, twin)
    trace_rows = table[: steps * receivers].reshape(steps, receivers)
    at = steps * receivers
    wave_row = table[at : at + steps]
    at += steps
    rec_x = table[at : at + receivers].astype(jnp.int32)
    rec_y = table[at + receivers : at + 2 * receivers].astype(jnp.int32)
    at += 2 * receivers
    src_x, src_y = table[at].astype(jnp.int32), table[at + 1].astype(jnp.int32)
    twin_anchor = twin[at + 2].astype(jnp.int32)
    anchors = (jnp.where(core == 0, anchor, twin_anchor), jnp.where(core == 0, twin_anchor, anchor))

    window = lay.start(chip_id) + lay.shift(core) - lay.pad[0]
    row_ids = jnp.arange(lay.width)
    line_ids = window + jnp.arange(lay.span)
    spread = ((0, 0), (0, 0), (0, z_count - steps))
    spot = (row_ids[:, None] == src_x) & (line_ids[None, :] == src_y)
    source_pulse = jnp.where(spot[:, :, None], wave_row[None, None, :], 0.0)
    receiver_pulse = jnp.einsum(
        "yr,xtr->xyt",
        (line_ids[:, None] == rec_y[None, :]).astype(jnp.float32),
        jnp.where((row_ids[:, None] == rec_x[None, :])[:, None, :], trace_rows[None], 0.0),
        precision=lax.Precision.HIGHEST,
        preferred_element_type=jnp.float32,
    )
    source_pulse = jnp.pad(source_pulse, spread)
    receiver_pulse = jnp.pad(receiver_pulse, spread)

    info = jnp.stack([chip_id, core, lay.shift(core)]).astype(jnp.int32)
    block = (lay.width, lay.span, z_count)
    state = pltpu.VMEM((2, 2, lay.width + 2, lay.span + 2 * TILE, z_count), jnp.float32)
    coefs, history = call(
        source_kernel,
        lay,
        [jax.ShapeDtypeStruct((COEFS,) + block, jnp.float32), jax.ShapeDtypeStruct((steps,) + block, jnp.float32)],
        [pltpu.VMEM((5,) + block, jnp.float32), state],
        info,
        source_pulse,
        *waves,
        *models,
    )
    image = call(
        receiver_kernel,
        lay,
        jax.ShapeDtypeStruct(block, jnp.float32),
        [state],
        info,
        receiver_pulse,
        coefs,
        history,
        *waves,
        *olds,
    )

    skip = (2 * chip_id + core) * lay.own - window
    frame = jnp.zeros((rows, shots * slab, z_count), jnp.float32)
    for r in range(domain):
        piece = lax.dynamic_slice(
            image, (lax.rem(d + r, domain) * rows, skip, zero), (rows, lay.own, z_count)
        )
        if r:
            piece = lax.ppermute(piece, "domain", [(i, (i + r) % domain) for i in range(domain)])
        source = lax.rem(d - r + domain, domain)
        place = jnp.where(source < lay.half, anchors[0], anchors[1])
        place = place + (2 * lax.rem(source, lay.half) + core) * lay.own
        spot = (zero, place, zero)
        frame = lax.dynamic_update_slice(
            frame, piece + lax.dynamic_slice(frame, spot, piece.shape), spot
        )
    total = 0.0
    for r in range(shots):
        part = lax.dynamic_slice_in_dim(frame, slab_owner[s ^ r] * slab, slab, 1)
        total = total + (swapped(part, "shot", r) if r else part)
    return total / steps


def solution(mesh):
    in_specs = (
        P(("groups", "domain"), "shot", None),
        P(("groups", "domain"), "shot", None),
        P(("groups", "domain"), "shot", None),
        P(("groups", "domain"), "shot", None),
        P(("groups", "domain"), "shot", None),
        P(("groups", "shot")),
        P(("groups", "shot")),
        P(("groups", "shot")),
        P(("groups", "shot"), None),
        P(("groups", "shot"), None),
        P(("groups", "shot"), None),
        P(("groups", "shot"), None, None),
        P(("groups", "shot"), None, "domain", None, None),
        P(("groups", "shot"), None, "domain", None, None),
        P(("groups", "shot"), None, "domain", None, None),
        P(("groups", "shot"), None, "domain", None, None),
        P("groups"),
    )
    out_specs = P(("groups", "domain"), "shot", None)
    return jax.shard_map(
        per_device, mesh=mesh, in_specs=in_specs, out_specs=out_specs, check_vma=False
    )
```

```python
import functools

import jax
import jax.numpy as jnp
from jax import lax
from jax.experimental import pallas as pl
from jax.experimental.pallas import tpu as pltpu
from jax.sharding import PartitionSpec as P

SRC_Z = 3
REC_Z = 1
TILE = 8
COEFS = 16
LIMIT = 40 * 1024 * 1024


class Layout:
    def __init__(self, domain, shots, rows, lines, steps):
        self.domain, self.shots, self.rows, self.lines, self.steps = domain, shots, rows, lines, steps
        self.half = domain // 2
        self.part = rows // 2
        self.width = rows * domain
        self.own = lines // domain
        halo = -(-steps // TILE) * TILE
        if self.half == 2 and self.own % TILE == 0:
            self.pad = (0, 0)
            self.chip = 2 * self.own + halo
            self.stride = lines - self.chip
            self.span = self.own + 2 * halo
        else:
            self.chip = -(-(2 * self.own + 2 * halo) // TILE) * TILE
            self.pad = (halo, max(0, (self.half - 1) * 2 * self.own + self.chip - halo - lines))
            self.stride = 2 * self.own
            self.span = self.chip

    def start(self, kc):
        return kc * self.stride

    def shift(self, c):
        return c * (self.chip - self.span)

    def rounds(self):
        count = self.domain * self.shots
        for r in range(self.domain):
            pairs = []
            for d in range(self.domain):
                for s in range(self.shots):
                    k = (d + r) % self.domain
                    to_d = self.half * (s & 1) + (k >> 1)
                    to_s = (s & ~1) | (k & 1)
                    pairs.append((d * self.shots + s, to_d * self.shots + to_s))
            assert len({pair[1] for pair in pairs}) == count
            yield r, pairs


def swapped(value, axis, bit):
    count = lax.axis_size(axis)
    return lax.ppermute(value, axis, [(i, i ^ bit) for i in range(count)])


def swapped_round(value, axis, r):
    count = lax.axis_size(axis)
    return lax.ppermute(value, axis, [(i, (i + r) % count) for i in range(count)])


def gather_rows(info_ref, lay, own_refs, other_ref, store):
    kc, c = info_ref[0], info_ref[1]
    window = pl.ds(pl.multiple_of(info_ref[2], TILE), lay.span)
    for core, local in ((c, True), (1 - c, False)):
        k = 2 * kc + core
        for r in range(lay.domain):
            source = lax.rem(k - r + lay.domain, lay.domain)
            for part in range(lay.part):
                ref = own_refs[r].at[:, part, window, :] if local else other_ref.at[r, :, part]
                store(source * lay.rows + core * lay.part + part, ref)


def make_coefs(raw_ref, coef_ref, lay):
    lane = lax.broadcasted_iota(jnp.int32, (lay.span, raw_ref.shape[-1]), 1)
    last = raw_ref.shape[-1] - 1

    def from_below(value):
        return jnp.where(lane == 0, 0.0, pltpu.roll(value, 1, 1))

    def from_above(value):
        return jnp.where(lane == last, 0.0, pltpu.roll(value, last, 1))

    def one_row(row, unused):
        velocity, eps, delta, tilt, azimuth = (raw_ref[i, row] for i in range(5))
        gain_eps = 1.0 + 2.0 * eps
        gain_delta = jnp.sqrt(1.0 + 2.0 * delta)
        sin_tilt = jnp.sin(tilt)
        n_x = sin_tilt * jnp.cos(azimuth)
        n_y = sin_tilt * jnp.sin(azimuth)
        n_z = jnp.cos(tilt)
        xx, yy, zz = n_x * n_x, n_y * n_y, n_z * n_z
        xz, yz = 0.5 * n_x * n_z, 0.5 * n_y * n_z
        values = (
            xx, 1.0 - xx, yy, 1.0 - yy, 0.5 * n_x * n_y,
            from_below(zz), from_below(1.0 - zz), from_below(xz), from_below(yz),
            from_above(zz), from_above(1.0 - zz), from_above(xz), from_above(yz),
            velocity * gain_eps, velocity * gain_delta, velocity,
        )
        for i, value in enumerate(values):
            coef_ref[i, row] = value
        return unused

    lax.fori_loop(0, lay.width, one_row, 0)


def run_steps(state, coef_ref, inject_ref, depth, lay, after):
    z_count = state.shape[-1]
    last = z_count - 1
    lane = lax.broadcasted_iota(jnp.int32, (TILE, z_count), 1)
    chunk = next(size for size in (8, 4, 2, 1) if lay.width % size == 0)

    def row_of(now, field, row, tile):
        base = TILE + TILE * tile
        middle = state[now, field, row, base : base + TILE, :]
        low = state[now, field, row, base - 1 : base - 1 + TILE, :]
        high = state[now, field, row, base + 1 : base + 1 + TILE, :]
        return middle, high - low, high + low

    def one_step(step, unused):
        now = lax.rem(step, 2)
        new = 1 - now
        turn = lax.rem(depth - step + z_count, z_count)

        def one_chunk(first):
            for tile in range(lay.span // TILE):
                lines = slice(TILE * tile, TILE * tile + TILE)
                inner = slice(TILE + TILE * tile, 2 * TILE + TILE * tile)
                before = [row_of(now, field, first, tile) for field in (0, 1)]
                here = [row_of(now, field, first + 1, tile) for field in (0, 1)]
                for i in range(chunk):
                    row = first + i
                    beyond = [row_of(now, field, row + 2, tile) for field in (0, 1)]
                    coef = [coef_ref[n, row, lines, :] for n in range(COEFS)]
                    xx, xx0, yy, yy0, xy = coef[:5]
                    zz_b, zz0_b, xz_b, yz_b, zz_a, zz0_a, xz_a, yz_a = coef[5:13]
                    axial_gain, cross_gain, velocity = coef[13:]

                    def terms(field):
                        f, diff_y, sum_y = here[field]
                        sum_x = beyond[field][0] + before[field][0]
                        diff_x = beyond[field][0] - before[field][0]
                        mixed = beyond[field][1] - before[field][1]
                        below = xz_b * diff_x + yz_b * diff_y
                        above = xz_a * diff_x + yz_a * diff_y
                        return f, sum_x, sum_y, xy * mixed, below, above

                    p, sum_x, sum_y, mixed, below, above = terms(0)
                    across = xx0 * sum_x + yy0 * sum_y - mixed
                    across += pltpu.roll(zz0_b * p - below, last, 1) + pltpu.roll(zz0_a * p + above, 1, 1)
                    across -= 4.0 * p
                    q, sum_x, sum_y, mixed, below, above = terms(1)
                    axial = xx * sum_x + yy * sum_y + mixed
                    axial += pltpu.roll(zz_b * q + below, last, 1) + pltpu.roll(zz_a * q - above, 1, 1)
                    axial -= 2.0 * q
                    pulse = pltpu.roll(inject_ref[row, lines, :], turn, 1)
                    pulse = velocity * jnp.where(lane == depth, pulse, 0.0)
                    old_p = state[new, 0, row + 1, inner, :]
                    old_q = state[new, 1, row + 1, inner, :]
                    new_p = (p + p - old_p) + (axial_gain * across + cross_gain * axial) + pulse
                    new_q = (q + q - old_q) + (cross_gain * across + velocity * axial) + pulse
                    state[new, 0, row + 1, inner, :] = new_p
                    state[new, 1, row + 1, inner, :] = new_q
                    after(step, row, lines, new_p)
                    before, here = here, beyond

        if chunk == lay.width:
            one_chunk(0)
        else:
            lax.fori_loop(0, lay.width // chunk, lambda n, u: (one_chunk(n * chunk), u)[1], 0)
        return unused

    lax.fori_loop(0, lay.steps, one_step, 0)


def clear_edges(state, lay):
    rows, lines = state.shape[2], state.shape[3]
    edge = jnp.zeros((lines,) + state.shape[4:], jnp.float32)
    strip = jnp.zeros((rows, TILE) + state.shape[4:], jnp.float32)
    for time in (0, 1):
        for field in (0, 1):
            state[time, field, 0] = edge
            state[time, field, rows - 1] = edge
            state[time, field, :, :TILE] = strip
            state[time, field, :, lines - TILE :] = strip


def source_kernel(lay, info_ref, inject_ref, waves_other, model_other, *refs):
    count = lay.domain
    coef_ref, history_ref, raw, state = refs[2 * count :]
    clear_edges(state, lay)

    def store_wave(row, ref):
        for time in (0, 1):
            for field in (0, 1):
                state[time, field, row + 1, TILE : TILE + lay.span, :] = ref[2 * time + field]

    def store_model(row, ref):
        for i in range(5):
            raw[i, row] = ref[i]

    gather_rows(info_ref, lay, refs[:count], waves_other, store_wave)
    gather_rows(info_ref, lay, refs[count : 2 * count], model_other, store_model)
    make_coefs(raw, coef_ref, lay)

    def after(step, row, lines, new_p):
        history_ref[step, row, lines, :] = new_p

    run_steps(state, coef_ref, inject_ref, SRC_Z, lay, after)


def receiver_kernel(lay, info_ref, inject_ref, coef_ref, history_ref, waves_other, old_other, *refs):
    count = lay.domain
    pieces, (image_ref, state) = refs[2 * count : 3 * count], refs[3 * count :]
    clear_edges(state, lay)

    def store_now(row, ref):
        for field in (0, 1):
            state[0, field, row + 1, TILE : TILE + lay.span, :] = ref[4 + field]

    def store_old(row, ref):
        for field in (0, 1):
            state[1, field, row + 1, TILE : TILE + lay.span, :] = ref[field]

    gather_rows(info_ref, lay, refs[:count], waves_other, store_now)
    gather_rows(info_ref, lay, refs[count : 2 * count], old_other, store_old)
    image_ref[...] = jnp.zeros_like(image_ref)

    def after(step, row, lines, new_p):
        image_ref[row, lines, :] += history_ref[step, row, lines, :] * new_p

    run_steps(state, coef_ref, inject_ref, REC_Z, lay, after)
    d, skip = info_ref[3], info_ref[4]
    if lay.own % TILE == 0:
        skip = pl.multiple_of(skip, TILE)
    for r, piece in enumerate(pieces):
        first = lax.rem(d + r, lay.domain) * lay.rows
        for row in range(lay.rows):
            if lay.own % TILE == 0:
                piece[row] = image_ref[first + row, pl.ds(skip, lay.own), :]
            else:
                piece[row] = pltpu.roll(image_ref[first + row], lay.span - skip, 0)[: lay.own]


def pack_kernel(lay, info_ref, *refs, sources, models):
    fields, arrays = refs[:sources], refs[sources : sources + models]
    outs, sem = refs[len(refs) - 1 - lay.domain - (models > 0) : -1], refs[-1]
    copies = []
    for r in range(lay.domain):
        k = lax.rem(info_ref[3] + r, lay.domain)
        rows = pl.ds((k & 1) * lay.part, lay.part)
        lines = pl.ds(pl.multiple_of((k >> 1) * lay.stride, TILE), lay.chip)
        for i, field in enumerate(fields):
            copies.append((field.at[:, rows, lines, :], outs[r].at[2 * i : 2 * i + 2]))
    for i, array in enumerate(arrays):
        copies.append((array, outs[lay.domain].at[i]))
    copies = [pltpu.make_async_copy(source, target, sem.at[i]) for i, (source, target) in enumerate(copies)]
    for copy in copies:
        copy.start()
    for copy in copies:
        copy.wait()


def pack(lay, info, fields, arrays, after):
    anywhere = pl.BlockSpec(memory_space=pl.ANY)
    z_count = fields[0].shape[-1]
    outs = [jax.ShapeDtypeStruct((2 * len(fields), lay.part, lay.chip, z_count), jnp.float32)] * lay.domain
    if arrays:
        outs.append(jax.ShapeDtypeStruct((len(arrays),) + arrays[0].shape, jnp.float32))
    operands = list(fields) + list(arrays) + list(after)
    return pl.pallas_call(
        functools.partial(pack_kernel, lay, sources=len(fields), models=len(arrays)),
        out_shape=outs,
        in_specs=[pl.BlockSpec(memory_space=pltpu.SMEM)] + [anywhere] * len(operands),
        out_specs=[anywhere] * len(outs),
        scratch_shapes=[pltpu.SemaphoreType.DMA((lay.domain * len(fields) + len(arrays),))],
    )(info, *operands)


def frame_kernel(lay, info_ref, *refs, slab):
    pieces, outs, frame = refs[: lay.domain], refs[lay.domain : -1], refs[-1]
    frame[...] = jnp.zeros_like(frame)
    room = -(-lay.own // TILE) * TILE + TILE
    filler = jnp.zeros((room - lay.own, frame.shape[-1]), jnp.float32)
    for r, piece in enumerate(pieces):
        place = info_ref[r]
        first = pl.multiple_of(place & ~(TILE - 1), TILE)
        for row in range(lay.rows):
            moved = pltpu.roll(jnp.concatenate([piece[row], filler]), place & (TILE - 1), 0)
            frame[row, pl.ds(first, room), :] += moved
    for r, out in enumerate(outs):
        first = pl.multiple_of(info_ref[lay.domain + r] * slab, TILE)
        for row in range(lay.rows):
            out[row] = frame[row, pl.ds(first, slab), :]


def call(kernel, lay, outs, scratch, info, *operands):
    vmem = pl.BlockSpec(memory_space=pltpu.VMEM)
    return pl.pallas_call(
        functools.partial(kernel, lay),
        out_shape=outs,
        in_specs=[pl.BlockSpec(memory_space=pltpu.SMEM)] + [vmem] * len(operands),
        out_specs=jax.tree.map(lambda unused: vmem, outs),
        scratch_shapes=scratch,
        compiler_params=pltpu.CompilerParams(vmem_limit_bytes=LIMIT),
    )(info, *operands)


def per_device(
    velocity,
    thomsen_eps,
    thomsen_delta,
    tilt_angle,
    azimuth,
    shot_anchor,
    source_x,
    source_y,
    wavelet,
    receiver_x,
    receiver_y,
    traces,
    source_now,
    source_before,
    receiver_now,
    receiver_before,
    slab_owner,
):
    rows, lines, z_count = source_now.shape[2:]
    steps = wavelet.shape[1]
    domain, shots = lax.axis_size("domain"), lax.axis_size("shot")
    lay = Layout(domain, shots, rows, lines, steps)
    d, s = lax.axis_index("domain"), lax.axis_index("shot")
    core = s & 1
    chip_id = lax.rem(d, lay.half)
    works_on = d // lay.half
    zero = jnp.int32(0)

    window = lay.start(chip_id) + lay.shift(core) - lay.pad[0]
    skip = (2 * chip_id + core) * lay.own - window
    info = jnp.stack([chip_id, core, lay.shift(core), d, skip]).astype(jnp.int32)
    tight = lay.pad == (0, 0)

    def wave_messages(fields, arrays=(), after=()):
        fields = [field[0] for field in fields]
        if tight:
            return pack(lay, info, fields, arrays, after)
        fields = [jnp.pad(field, ((0, 0), (0, 0), lay.pad, (0, 0))) for field in fields]
        messages = []
        for r in range(domain):
            k = lax.rem(d + r, domain)
            spot = (zero, (k & 1) * lay.part, lay.start(k >> 1), zero)
            size = (2, lay.part, lay.chip, z_count)
            messages.append(jnp.concatenate([lax.dynamic_slice(field, spot, size) for field in fields]))
        return messages + ([jnp.stack(arrays)] if arrays else [])

    def send(messages):
        return [lax.ppermute(messages[r], ("domain", "shot"), pairs) for r, pairs in lay.rounds()]

    def other_core(messages):
        cut = lay.shift(1 - core)
        return swapped(
            jnp.stack([lax.dynamic_slice_in_dim(message, cut, lay.span, 2) for message in messages]), "shot", 1
        )

    *messages, model = wave_messages(
        (source_now, source_before, receiver_now), (velocity, thomsen_eps, thomsen_delta, tilt_angle, azimuth)
    )
    waves = send(messages)

    slab = model.shape[2]
    model = model[:, :, None]
    bit = shots // 2
    while bit:
        twin = swapped(model, "shot", bit)
        upper = (s & bit) != 0
        model = jnp.stack([jnp.where(upper, twin, model), jnp.where(upper, model, twin)], axis=3)
        model = model.reshape(model.shape[:2] + (-1,) + model.shape[4:])
        bit //= 2
    model = model.reshape(model.shape[:2] + (shots * slab, z_count))
    anchor = shot_anchor[0]
    if tight:
        first_line = anchor
    else:
        model = lax.dynamic_slice_in_dim(model, anchor, lines, 2)
        model = jnp.pad(model, ((0, 0), (0, 0), lay.pad, (0, 0)))
        first_line = zero
    messages = []
    for r in range(domain):
        k = lax.rem(d + r, domain)
        spot = (zero, (k & 1) * lay.part, first_line + lay.start(k >> 1), zero)
        messages.append(lax.dynamic_slice(model, spot, (5, lay.part, lay.chip, z_count)))
    models = send(messages)
    olds = send(wave_messages((receiver_before,), after=models[1:2]))
    waves_other, models_other, olds_other = other_core(waves), other_core(models), other_core(olds)

    receivers = receiver_x.shape[1]
    mine = jnp.concatenate(
        [
            traces[0].reshape(-1),
            wavelet[0],
            receiver_x[0].astype(jnp.float32),
            receiver_y[0].astype(jnp.float32),
            source_x.astype(jnp.float32),
            source_y.astype(jnp.float32),
            shot_anchor.astype(jnp.float32),
        ]
    )
    twin = swapped(mine, "shot", 1)
    table = jnp.where(works_on == core, mine, twin)
    trace_rows = table[: steps * receivers].reshape(steps, receivers)
    at = steps * receivers
    wave_row = table[at : at + steps]
    at += steps
    rec_x = table[at : at + receivers].astype(jnp.int32)
    rec_y = table[at + receivers : at + 2 * receivers].astype(jnp.int32)
    at += 2 * receivers
    src_x, src_y = table[at].astype(jnp.int32), table[at + 1].astype(jnp.int32)
    twin_anchor = twin[at + 2].astype(jnp.int32)
    anchors = (jnp.where(core == 0, anchor, twin_anchor), jnp.where(core == 0, twin_anchor, anchor))

    row_ids = jnp.arange(lay.width)
    line_ids = window + jnp.arange(lay.span)
    spread = ((0, 0), (0, 0), (0, z_count - steps))
    spot = (row_ids[:, None] == src_x) & (line_ids[None, :] == src_y)
    source_pulse = jnp.where(spot[:, :, None], wave_row[None, None, :], 0.0)
    receiver_pulse = jnp.einsum(
        "yr,xtr->xyt",
        (line_ids[:, None] == rec_y[None, :]).astype(jnp.float32),
        jnp.where((row_ids[:, None] == rec_x[None, :])[:, None, :], trace_rows[None], 0.0),
        precision=lax.Precision.HIGHEST,
        preferred_element_type=jnp.float32,
    )
    source_pulse = jnp.pad(source_pulse, spread)
    receiver_pulse = jnp.pad(receiver_pulse, spread)

    block = (lay.width, lay.span, z_count)
    state = pltpu.VMEM((2, 2, lay.width + 2, lay.span + 2 * TILE, z_count), jnp.float32)
    coefs, history = call(
        source_kernel,
        lay,
        [jax.ShapeDtypeStruct((COEFS,) + block, jnp.float32), jax.ShapeDtypeStruct((steps,) + block, jnp.float32)],
        [pltpu.VMEM((5,) + block, jnp.float32), state],
        info,
        source_pulse,
        waves_other,
        models_other,
        *waves,
        *models,
    )
    pieces = call(
        receiver_kernel,
        lay,
        [jax.ShapeDtypeStruct((rows, lay.own, z_count), jnp.float32)] * domain,
        [pltpu.VMEM(block, jnp.float32), state],
        info,
        receiver_pulse,
        coefs,
        history,
        waves_other,
        olds_other,
        *waves,
        *olds,
    )

    source = lax.rem(d - jnp.arange(domain) + domain, domain)
    places = jnp.where(source < lay.half, anchors[0], anchors[1])
    places = places + (2 * lax.rem(source, lay.half) + core) * lay.own
    owners = slab_owner[s ^ jnp.arange(shots)]
    pieces = [
        swapped_round(piece, "domain", r) if r else piece for r, piece in enumerate(pieces)
    ]
    room = -(-lay.own // TILE) * TILE + TILE
    parts = call(
        functools.partial(frame_kernel, slab=slab),
        lay,
        [jax.ShapeDtypeStruct((rows, slab, z_count), jnp.float32)] * shots,
        [pltpu.VMEM((rows, shots * slab + room, z_count), jnp.float32)],
        jnp.concatenate([places, owners]).astype(jnp.int32),
        *pieces,
    )
    total = parts[0]
    for r in range(1, shots):
        total = total + swapped(parts[r], "shot", r)
    return total / steps


def solution(mesh):
    in_specs = (
        P(("groups", "domain"), "shot", None),
        P(("groups", "domain"), "shot", None),
        P(("groups", "domain"), "shot", None),
        P(("groups", "domain"), "shot", None),
        P(("groups", "domain"), "shot", None),
        P(("groups", "shot")),
        P(("groups", "shot")),
        P(("groups", "shot")),
        P(("groups", "shot"), None),
        P(("groups", "shot"), None),
        P(("groups", "shot"), None),
        P(("groups", "shot"), None, None),
        P(("groups", "shot"), None, "domain", None, None),
        P(("groups", "shot"), None, "domain", None, None),
        P(("groups", "shot"), None, "domain", None, None),
        P(("groups", "shot"), None, "domain", None, None),
        P("groups"),
    )
    out_specs = P(("groups", "domain"), "shot", None)
    return jax.shard_map(
        per_device, mesh=mesh, in_specs=in_specs, out_specs=out_specs, check_vma=False
    )
```

```python
import functools
import math

import jax
import jax.numpy as jnp
from jax import lax
from jax.experimental import pallas as pl
from jax.experimental.pallas import tpu as pltpu
from jax.sharding import PartitionSpec as P

SRC_Z = 3
REC_Z = 1
TILE = 8
COEFS = 16


class Layout:
    def __init__(self, domain, shots, rows, lines, steps):
        self.domain, self.shots, self.rows, self.lines, self.steps = domain, shots, rows, lines, steps
        self.half = domain // 2
        self.part = rows // 2
        self.width = rows * domain
        self.own = lines // domain
        halo = -(-steps // TILE) * TILE
        if self.half == 2 and self.own % TILE == 0:
            self.pad = (0, 0)
            self.chip = 2 * self.own + halo
            self.stride = lines - self.chip
            self.span = self.own + 2 * halo
        else:
            self.chip = -(-(2 * self.own + 2 * halo) // TILE) * TILE
            self.pad = (halo, max(0, (self.half - 1) * 2 * self.own + self.chip - halo - lines))
            self.stride = 2 * self.own
            self.span = self.chip

    def start(self, kc):
        return kc * self.stride

    def shift(self, c):
        return c * (self.chip - self.span)

    def rounds(self):
        count = self.domain * self.shots
        for r in range(self.domain):
            pairs = []
            for d in range(self.domain):
                for s in range(self.shots):
                    k = (d + r) % self.domain
                    to_d = self.half * (s & 1) + (k >> 1)
                    to_s = (s & ~1) | (k & 1)
                    pairs.append((d * self.shots + s, to_d * self.shots + to_s))
            assert len({pair[1] for pair in pairs}) == count
            yield r, pairs


def swapped(value, axis, bit):
    count = lax.axis_size(axis)
    return lax.ppermute(value, axis, [(i, i ^ bit) for i in range(count)])


def tied(value, *others):
    return lax.optimization_barrier((value, *others))[0]


def swapped_round(value, axis, r):
    count = lax.axis_size(axis)
    return lax.ppermute(value, axis, [(i, (i + r) % count) for i in range(count)])


def gather_rows(info_ref, lay, own_refs, other_refs, store):
    kc, c = info_ref[0], info_ref[1]
    window = pl.ds(pl.multiple_of(info_ref[2], TILE), lay.span)
    for core, refs in ((c, own_refs), (1 - c, other_refs)):
        k = 2 * kc + core
        for r, ref in enumerate(refs):
            source = lax.rem(k - r + lay.domain, lay.domain)
            for part in range(lay.part):
                store(source * lay.rows + core * lay.part + part, ref.at[:, part, window, :])


def make_coefs(raw_ref, coef_ref, lay):
    lane = lax.broadcasted_iota(jnp.int32, (lay.span, raw_ref.shape[-1]), 1)
    last = raw_ref.shape[-1] - 1

    def from_below(value):
        return jnp.where(lane == 0, 0.0, pltpu.roll(value, 1, 1))

    def from_above(value):
        return jnp.where(lane == last, 0.0, pltpu.roll(value, last, 1))

    def one_row(row, unused):
        velocity, eps, delta, tilt, azimuth = (raw_ref[i, row] for i in range(5))
        gain_eps = 1.0 + 2.0 * eps
        gain_delta = jnp.sqrt(1.0 + 2.0 * delta)
        sin_tilt = jnp.sin(tilt)
        n_x = sin_tilt * jnp.cos(azimuth)
        n_y = sin_tilt * jnp.sin(azimuth)
        n_z = jnp.cos(tilt)
        xx, yy, zz = n_x * n_x, n_y * n_y, n_z * n_z
        xz, yz = 0.5 * n_x * n_z, 0.5 * n_y * n_z
        values = (
            xx, 1.0 - xx, yy, 1.0 - yy, 0.5 * n_x * n_y,
            from_below(zz), from_below(1.0 - zz), from_below(xz), from_below(yz),
            from_above(zz), from_above(1.0 - zz), from_above(xz), from_above(yz),
            velocity * gain_eps, velocity * gain_delta, velocity,
        )
        for i, value in enumerate(values):
            coef_ref[i, row] = value
        return unused

    lax.fori_loop(0, lay.width, one_row, 0)


def run_steps(state, coef_ref, inject_refs, image_ref, lay):
    z_count = state.shape[-1]
    last = z_count - 1
    lane = lax.broadcasted_iota(jnp.int32, (TILE, z_count), 1)
    chunk = next(size for size in (8, 4, 2, 1) if lay.width % size == 0)

    def row_of(now, field, row, tile):
        base = TILE + TILE * tile
        middle = state[now, field, row, base : base + TILE, :]
        low = state[now, field, row, base - 1 : base - 1 + TILE, :]
        high = state[now, field, row, base + 1 : base + 1 + TILE, :]
        return middle, high - low, high + low

    def sweep(step, now, new, first, tile, wave):
        depth = (SRC_Z, REC_Z)[wave]
        turn = lax.rem(depth - step + z_count, z_count)
        lines = slice(TILE * tile, TILE * tile + TILE)
        inner = slice(TILE + TILE * tile, 2 * TILE + TILE * tile)
        pair = (2 * wave, 2 * wave + 1)
        before = [row_of(now, field, first, tile) for field in pair]
        here = [row_of(now, field, first + 1, tile) for field in pair]
        for i in range(chunk):
            row = first + i
            beyond = [row_of(now, field, row + 2, tile) for field in pair]
            coef = [coef_ref[n, row, lines, :] for n in range(COEFS)]
            xx, xx0, yy, yy0, xy = coef[:5]
            zz_b, zz0_b, xz_b, yz_b, zz_a, zz0_a, xz_a, yz_a = coef[5:13]
            axial_gain, cross_gain, velocity = coef[13:]

            def terms(field):
                f, diff_y, sum_y = here[field]
                sum_x = beyond[field][0] + before[field][0]
                diff_x = beyond[field][0] - before[field][0]
                mixed = beyond[field][1] - before[field][1]
                below = xz_b * diff_x + yz_b * diff_y
                above = xz_a * diff_x + yz_a * diff_y
                return f, sum_x, sum_y, xy * mixed, below, above

            p, sum_x, sum_y, mixed, below, above = terms(0)
            across = xx0 * sum_x + yy0 * sum_y - mixed
            across += pltpu.roll(zz0_b * p - below, last, 1) + pltpu.roll(zz0_a * p + above, 1, 1)
            across -= 4.0 * p
            q, sum_x, sum_y, mixed, below, above = terms(1)
            axial = xx * sum_x + yy * sum_y + mixed
            axial += pltpu.roll(zz_b * q + below, last, 1) + pltpu.roll(zz_a * q - above, 1, 1)
            axial -= 2.0 * q
            pulse = pltpu.roll(inject_refs[wave][row, lines, :], turn, 1)
            pulse = velocity * jnp.where(lane == depth, pulse, 0.0)
            old_p = state[new, pair[0], row + 1, inner, :]
            old_q = state[new, pair[1], row + 1, inner, :]
            new_p = (p + p - old_p) + (axial_gain * across + cross_gain * axial) + pulse
            new_q = (q + q - old_q) + (cross_gain * across + velocity * axial) + pulse
            state[new, pair[0], row + 1, inner, :] = new_p
            state[new, pair[1], row + 1, inner, :] = new_q
            if wave == 1:
                image_ref[row, lines, :] += state[new, 0, row + 1, inner, :] * new_p
            before, here = here, beyond

    def one_step(step, unused):
        now = lax.rem(step, 2)

        def one_chunk(first):
            for tile in range(lay.span // TILE):
                for wave in (0, 1):
                    sweep(step, now, 1 - now, first, tile, wave)

        if chunk == lay.width:
            one_chunk(0)
        else:
            lax.fori_loop(0, lay.width // chunk, lambda n, u: (one_chunk(n * chunk), u)[1], 0)
        return unused

    lax.fori_loop(0, lay.steps, one_step, 0)


def clear_edges(state, lay):
    rows, lines = state.shape[2], state.shape[3]
    edge = jnp.zeros((lines,) + state.shape[4:], jnp.float32)
    strip = jnp.zeros((rows, TILE) + state.shape[4:], jnp.float32)
    for time in range(state.shape[0]):
        for field in range(state.shape[1]):
            state[time, field, 0] = edge
            state[time, field, rows - 1] = edge
            state[time, field, :, :TILE] = strip
            state[time, field, :, lines - TILE :] = strip


def wave_kernel(lay, info_ref, source_ref, receiver_ref, *refs):
    waves_own, waves_other, model_own, model_other, pieces = (
        refs[i * lay.domain : (i + 1) * lay.domain] for i in range(5)
    )
    raw, coef_ref, image_ref, state = refs[5 * lay.domain :]
    clear_edges(state, lay)

    def store_wave(row, ref):
        for i in range(8):
            time, field = (i >> 1) & 1, 2 * (i >> 2) + (i & 1)
            state[time, field, row + 1, TILE : TILE + lay.span, :] = ref[i]

    def store_model(row, ref):
        for i in range(5):
            raw[i, row] = ref[i]

    gather_rows(info_ref, lay, waves_own, waves_other, store_wave)
    gather_rows(info_ref, lay, model_own, model_other, store_model)
    make_coefs(raw, coef_ref, lay)
    image_ref[...] = jnp.zeros_like(image_ref)
    run_steps(state, coef_ref, (source_ref, receiver_ref), image_ref, lay)
    d, skip = info_ref[3], info_ref[4]
    if lay.own % TILE == 0:
        skip = pl.multiple_of(skip, TILE)
    for r, piece in enumerate(pieces):
        first = lax.rem(d + r, lay.domain) * lay.rows
        for row in range(lay.rows):
            if lay.own % TILE == 0:
                piece[row] = image_ref[first + row, pl.ds(skip, lay.own), :]
            else:
                piece[row] = pltpu.roll(image_ref[first + row], lay.span - skip, 0)[: lay.own]


def stack_kernel(*refs):
    *arrays, out, sem = refs
    copies = [pltpu.make_async_copy(array, out.at[i], sem.at[i]) for i, array in enumerate(arrays)]
    for copy in copies:
        copy.start()
    for copy in copies:
        copy.wait()


def stacked(arrays):
    return pl.pallas_call(
        stack_kernel,
        out_shape=jax.ShapeDtypeStruct((len(arrays),) + arrays[0].shape, jnp.float32),
        in_specs=[pl.BlockSpec(memory_space=pl.ANY)] * len(arrays),
        out_specs=pl.BlockSpec(memory_space=pltpu.VMEM),
        scratch_shapes=[pltpu.SemaphoreType.DMA((len(arrays),))],
    )(*arrays)


def frame_kernel(lay, info_ref, *refs, slab):
    pieces, outs, frame = refs[: lay.domain], refs[lay.domain : -1], refs[-1]
    frame[...] = jnp.zeros_like(frame)
    room = -(-lay.own // TILE) * TILE + TILE
    filler = jnp.zeros((room - lay.own, frame.shape[-1]), jnp.float32)
    for r, piece in enumerate(pieces):
        place = info_ref[r]
        first = pl.multiple_of(place & ~(TILE - 1), TILE)
        for row in range(lay.rows):
            moved = pltpu.roll(jnp.concatenate([piece[row], filler]), place & (TILE - 1), 0)
            frame[row, pl.ds(first, room), :] += moved
    for r, out in enumerate(outs):
        first = pl.multiple_of(info_ref[lay.domain + r] * slab, TILE)
        for row in range(lay.rows):
            out[row] = frame[row, pl.ds(first, slab), :]


def call(kernel, cost, lay, outs, scratch, info, *operands):
    vmem = pl.BlockSpec(memory_space=pltpu.VMEM)
    held = sum(4 * math.prod(array.shape) for array in [*operands, *outs, *scratch])
    return pl.pallas_call(
        functools.partial(kernel, lay),
        out_shape=outs,
        in_specs=[pl.BlockSpec(memory_space=pltpu.SMEM)] + [vmem] * len(operands),
        out_specs=jax.tree.map(lambda unused: vmem, outs),
        scratch_shapes=scratch,
        compiler_params=pltpu.CompilerParams(vmem_limit_bytes=held + held // 8 + 2**21),
        cost_estimate=pl.CostEstimate(flops=0, bytes_accessed=cost, transcendentals=0),
    )(info, *operands)


def per_device(
    velocity,
    thomsen_eps,
    thomsen_delta,
    tilt_angle,
    azimuth,
    shot_anchor,
    source_x,
    source_y,
    wavelet,
    receiver_x,
    receiver_y,
    traces,
    source_now,
    source_before,
    receiver_now,
    receiver_before,
    slab_owner,
):
    rows, lines, z_count = source_now.shape[2:]
    steps = wavelet.shape[1]
    domain, shots = lax.axis_size("domain"), lax.axis_size("shot")
    lay = Layout(domain, shots, rows, lines, steps)
    d, s = lax.axis_index("domain"), lax.axis_index("shot")
    core = s & 1
    chip_id = lax.rem(d, lay.half)
    works_on = d // lay.half
    zero = jnp.int32(0)

    window = lay.start(chip_id) + lay.shift(core) - lay.pad[0]
    skip = (2 * chip_id + core) * lay.own - window
    info = jnp.stack([chip_id, core, lay.shift(core), d, skip]).astype(jnp.int32)
    tight = lay.pad == (0, 0)

    def wave_messages(fields):
        fields = [jnp.pad(field[0], ((0, 0), (0, 0), lay.pad, (0, 0))) for field in fields]
        messages = []
        for r in range(domain):
            k = lax.rem(d + r, domain)
            spot = (zero, (k & 1) * lay.part, lay.start(k >> 1), zero)
            size = (2, lay.part, lay.chip, z_count)
            messages.append(jnp.concatenate([lax.dynamic_slice(field, spot, size) for field in fields]))
        return messages

    def send(messages):
        return [lax.ppermute(messages[r], ("domain", "shot"), pairs) for r, pairs in lay.rounds()]

    def other_core(messages):
        return [swapped(message, "shot", 1) for message in messages]

    waves = send(wave_messages((source_now, source_before, receiver_now, receiver_before)))
    model = stacked((velocity, thomsen_eps, thomsen_delta, tilt_angle, azimuth))
    slab = model.shape[2]
    whole = jnp.zeros(model.shape[:2] + (shots * slab, z_count), jnp.float32)
    for r in range(shots):
        block = swapped(model, "shot", r) if r else model
        whole = lax.dynamic_update_slice(whole, block, (zero, zero, (s ^ r) * slab, zero))
    model = whole
    anchor = shot_anchor[0]
    if tight:
        first_line = anchor
    else:
        model = lax.dynamic_slice_in_dim(model, anchor, lines, 2)
        model = jnp.pad(model, ((0, 0), (0, 0), lay.pad, (0, 0)))
        first_line = zero
    messages = []
    for r in range(domain):
        k = lax.rem(d + r, domain)
        spot = (zero, (k & 1) * lay.part, first_line + lay.start(k >> 1), zero)
        messages.append(lax.dynamic_slice(model, spot, (5, lay.part, lay.chip, z_count)))
    *messages, waves[-1] = lax.optimization_barrier((*messages, waves[-1]))
    models = send(messages)
    *waves, models[0] = lax.optimization_barrier((*waves, models[0]))
    waves_other, models_other = other_core(waves), other_core(models)

    receivers = receiver_x.shape[1]
    traces, wavelet, receiver_x, receiver_y, source_x, source_y, shot_anchor, unused = lax.optimization_barrier(
        (traces, wavelet, receiver_x, receiver_y, source_x, source_y, shot_anchor, waves[0])
    )
    mine = jnp.concatenate(
        [
            traces[0].reshape(-1),
            wavelet[0],
            receiver_x[0].astype(jnp.float32),
            receiver_y[0].astype(jnp.float32),
            source_x.astype(jnp.float32),
            source_y.astype(jnp.float32),
            shot_anchor.astype(jnp.float32),
        ]
    )
    twin = swapped(mine, "shot", 1)
    table = jnp.where(works_on == core, mine, twin)
    trace_rows = table[: steps * receivers].reshape(steps, receivers)
    at = steps * receivers
    wave_row = table[at : at + steps]
    at += steps
    rec_x = table[at : at + receivers].astype(jnp.int32)
    rec_y = table[at + receivers : at + 2 * receivers].astype(jnp.int32)
    at += 2 * receivers
    src_x, src_y = table[at].astype(jnp.int32), table[at + 1].astype(jnp.int32)
    twin_anchor = twin[at + 2].astype(jnp.int32)
    anchors = (jnp.where(core == 0, anchor, twin_anchor), jnp.where(core == 0, twin_anchor, anchor))

    row_ids = jnp.arange(lay.width)
    line_ids = window + jnp.arange(lay.span)
    spread = ((0, 0), (0, 0), (0, z_count - steps))
    spot = (row_ids[:, None] == src_x) & (line_ids[None, :] == src_y)
    source_pulse = jnp.where(spot[:, :, None], wave_row[None, None, :], 0.0)
    receiver_pulse = jnp.einsum(
        "yr,xtr->xyt",
        (line_ids[:, None] == rec_y[None, :]).astype(jnp.float32),
        jnp.where((row_ids[:, None] == rec_x[None, :])[:, None, :], trace_rows[None], 0.0),
        precision=lax.Precision.HIGHEST,
        preferred_element_type=jnp.float32,
    )
    source_pulse = jnp.pad(source_pulse, spread)
    receiver_pulse = jnp.pad(receiver_pulse, spread)

    block = (lay.width, lay.span, z_count)
    pieces = call(
        wave_kernel,
        60_000_000,
        lay,
        [jax.ShapeDtypeStruct((rows, lay.own, z_count), jnp.float32)] * domain,
        [
            pltpu.VMEM((5,) + block, jnp.float32),
            pltpu.VMEM((COEFS,) + block, jnp.float32),
            pltpu.VMEM(block, jnp.float32),
            pltpu.VMEM((2, 4, lay.width + 2, lay.span + 2 * TILE, z_count), jnp.float32),
        ],
        info,
        source_pulse,
        receiver_pulse,
        *waves,
        *waves_other,
        *models,
        *models_other,
    )

    source = lax.rem(d - jnp.arange(domain) + domain, domain)
    places = jnp.where(source < lay.half, anchors[0], anchors[1])
    places = places + (2 * lax.rem(source, lay.half) + core) * lay.own
    owners = slab_owner[s ^ jnp.arange(shots)]
    pieces = [
        swapped_round(piece, "domain", r) if r else piece for r, piece in enumerate(pieces)
    ]
    room = -(-lay.own // TILE) * TILE + TILE
    parts = call(
        functools.partial(frame_kernel, slab=slab),
        2_000_000,
        lay,
        [jax.ShapeDtypeStruct((rows, slab, z_count), jnp.float32)] * shots,
        [pltpu.VMEM((rows, shots * slab + room, z_count), jnp.float32)],
        jnp.concatenate([places, owners]).astype(jnp.int32),
        *pieces,
    )
    total = parts[0]
    for r in range(1, shots):
        total = total + swapped(parts[r], "shot", r)
    return total / steps


def solution(mesh):
    in_specs = (
        P(("groups", "domain"), "shot", None),
        P(("groups", "domain"), "shot", None),
        P(("groups", "domain"), "shot", None),
        P(("groups", "domain"), "shot", None),
        P(("groups", "domain"), "shot", None),
        P(("groups", "shot")),
        P(("groups", "shot")),
        P(("groups", "shot")),
        P(("groups", "shot"), None),
        P(("groups", "shot"), None),
        P(("groups", "shot"), None),
        P(("groups", "shot"), None, None),
        P(("groups", "shot"), None, "domain", None, None),
        P(("groups", "shot"), None, "domain", None, None),
        P(("groups", "shot"), None, "domain", None, None),
        P(("groups", "shot"), None, "domain", None, None),
        P("groups"),
    )
    out_specs = P(("groups", "domain"), "shot", None)
    return jax.shard_map(
        per_device, mesh=mesh, in_specs=in_specs, out_specs=out_specs, check_vma=False
    )
```

```python
import functools
import math

import jax
import jax.numpy as jnp
from jax import lax
from jax.experimental import pallas as pl
from jax.experimental.pallas import tpu as pltpu
from jax.sharding import PartitionSpec as P

SRC_Z = 3
REC_Z = 1
TILE = 8
COEFS = 16


class Layout:
    def __init__(self, domain, shots, rows, lines, steps):
        self.domain, self.shots, self.rows, self.lines, self.steps = domain, shots, rows, lines, steps
        self.half = domain // 2
        self.part = rows // 2
        self.width = rows * domain
        self.own = lines // domain
        halo = -(-steps // TILE) * TILE
        if self.half == 2 and self.own % TILE == 0:
            self.pad = (0, 0)
            self.chip = 2 * self.own + halo
            self.stride = lines - self.chip
            self.span = self.own + 2 * halo
        else:
            self.chip = -(-(2 * self.own + 2 * halo) // TILE) * TILE
            self.pad = (halo, max(0, (self.half - 1) * 2 * self.own + self.chip - halo - lines))
            self.stride = 2 * self.own
            self.span = self.chip

    def start(self, kc):
        return kc * self.stride

    def shift(self, c):
        return c * (self.chip - self.span)

    def position(self):
        d, s = lax.axis_index("domain"), lax.axis_index("shot")
        return lax.rem(d, self.half), s & 1, d, d // self.half

    def rounds(self):
        count = self.domain * self.shots
        for r in range(self.domain):
            pairs = []
            for d in range(self.domain):
                for s in range(self.shots):
                    k = (d + r) % self.domain
                    to_d = self.half * (s & 1) + (k >> 1)
                    to_s = (s & ~1) | (k & 1)
                    pairs.append((d * self.shots + s, to_d * self.shots + to_s))
            assert len({pair[1] for pair in pairs}) == count
            yield r, pairs


def swapped(value, axis, bit):
    count = lax.axis_size(axis)
    return lax.ppermute(value, axis, [(i, i ^ bit) for i in range(count)])


def tied(value, *others):
    return lax.optimization_barrier((value, *others))[0]


def swapped_round(value, axis, r):
    count = lax.axis_size(axis)
    return lax.ppermute(value, axis, [(i, (i + r) % count) for i in range(count)])


def gather_rows(lay, own_refs, other_refs, store):
    kc, c, unused, unused = lay.position()
    window = pl.ds(pl.multiple_of(lay.shift(c), TILE), lay.span)
    for core, refs in ((c, own_refs), (1 - c, other_refs)):
        k = 2 * kc + core
        for r, ref in enumerate(refs):
            source = lax.rem(k - r + lay.domain, lay.domain)
            for part in range(lay.part):
                store(source * lay.rows + core * lay.part + part, ref.at[:, part, window, :])


def table_kernel(traces, wavelet, rec_x, rec_y, src_x, src_y, anchor, table):
    steps = traces.shape[1]
    table[...] = jnp.zeros_like(table)
    table[:steps] = traces[0]
    table[steps : steps + 1, :steps] = wavelet[...]
    row = (1, table.shape[1])
    table[steps + 1 : steps + 2] = rec_x[...].astype(jnp.float32)
    table[steps + 2 : steps + 3] = rec_y[...].astype(jnp.float32)
    for i, scalar in enumerate((src_x, src_y, anchor)):
        table[steps + 3 + i : steps + 4 + i] = jnp.full(row, scalar[0], jnp.int32).astype(jnp.float32)


def table_of(*arrays):
    steps, receivers = arrays[0].shape[1:]
    smem, vmem = (pl.BlockSpec(memory_space=space) for space in (pltpu.SMEM, pltpu.VMEM))
    return pl.pallas_call(
        table_kernel,
        out_shape=jax.ShapeDtypeStruct((-(-(steps + 6) // TILE) * TILE, receivers), jnp.float32),
        in_specs=[vmem] * 4 + [smem] * 3,
        out_specs=vmem,
        compiler_params=pltpu.CompilerParams(vmem_limit_bytes=2**21),
    )(*arrays)


def pulse_kernel(lay, mine, twin, receiver_out, source_out, scalars, padded):
    kc, c, d, works_on = lay.position()
    steps, lanes = lay.steps, receiver_out.shape[-1]
    window = lay.start(kc) + lay.shift(c) - lay.pad[0]
    table = jnp.where(works_on == c, mine[...], twin[...])

    def scalar(values, row):
        return jnp.max(values[row : row + 1]).astype(jnp.int32)

    src_x, src_y = scalar(table, steps + 3), scalar(table, steps + 4) - window
    first = jnp.clip(src_y, 0, lay.span - 1) & ~(TILE - 1)
    anchors = scalar(mine[...], steps + 5), scalar(twin[...], steps + 5)
    scalars[0], scalars[1] = src_x, first
    scalars[2] = jnp.where(c == 0, anchors[0], anchors[1])
    scalars[3] = jnp.where(c == 0, anchors[1], anchors[0])

    lane = lax.broadcasted_iota(jnp.int32, (TILE, lanes), 1)
    line = lax.broadcasted_iota(jnp.int32, (TILE, lanes), 0)
    spot = (lane == SRC_Z) & (line + first == src_y)
    at_step = lax.broadcasted_iota(jnp.int32, (1, table.shape[1]), 1)
    for step in range(steps):
        amount = jnp.sum(jnp.where(at_step == step, table[steps : steps + 1], 0.0))
        source_out[step] = jnp.where(spot, amount, 0.0)

    lines = lax.broadcasted_iota(jnp.int32, (lay.span, table.shape[1]), 0) + window
    there = (lines == table[steps + 2 : steps + 3].astype(jnp.int32)).astype(jnp.float32)
    padded[...] = jnp.zeros_like(padded)

    def one_row(row, unused):
        here = table[steps + 1 : steps + 2].astype(jnp.int32) == row
        padded[:steps] = jnp.where(here, table[:steps], 0.0)
        receiver_out[row] = lax.dot_general(
            there,
            padded[...],
            (((1,), (1,)), ((), ())),
            precision=lax.Precision.HIGHEST,
            preferred_element_type=jnp.float32,
        )
        return unused

    lax.fori_loop(0, lay.width, one_row, 0)


def pulses(lay, mine, twin, z_count):
    shapes = [(lay.width, lay.span, z_count), (lay.steps, TILE, z_count)]
    held = 4 * (2 * math.prod(shapes[0]) + z_count * mine.shape[1])
    smem, vmem = (pl.BlockSpec(memory_space=space) for space in (pltpu.SMEM, pltpu.VMEM))
    return pl.pallas_call(
        functools.partial(pulse_kernel, lay),
        out_shape=[jax.ShapeDtypeStruct(shape, jnp.float32) for shape in shapes]
        + [jax.ShapeDtypeStruct((4,), jnp.int32)],
        in_specs=[vmem] * 2,
        out_specs=[vmem, vmem, smem],
        scratch_shapes=[pltpu.VMEM((z_count, mine.shape[1]), jnp.float32)],
        compiler_params=pltpu.CompilerParams(vmem_limit_bytes=held + 2**21),
    )(mine, twin)


def sin_cos(angle):
    square = angle * angle
    sine, cosine = 1.0 / 6227020800.0, -1.0 / 87178291200.0
    for n in (11, 9, 7, 5, 3, 1):
        sine = sine * square + (-1.0) ** (n // 2) / math.factorial(n)
    for n in (12, 10, 8, 6, 4, 2, 0):
        cosine = cosine * square + (-1.0) ** (n // 2) / math.factorial(n)
    return sine * angle, cosine


def medium_kernel(velocity, eps, delta, tilt, azimuth, out):
    speed = velocity[...]
    out[0] = speed
    out[1] = speed * (1.0 + 2.0 * eps[...])
    out[2] = speed * jnp.sqrt(1.0 + 2.0 * delta[...])
    sin_tilt, unused = sin_cos(tilt[...])
    sine, cosine = sin_cos(0.5 * azimuth[...])
    out[3] = sin_tilt * (1.0 - 2.0 * sine * sine)
    out[4] = sin_tilt * (2.0 * sine * cosine)


def medium(*arrays):
    vmem = pl.BlockSpec(memory_space=pltpu.VMEM)
    return pl.pallas_call(
        medium_kernel,
        out_shape=jax.ShapeDtypeStruct((len(arrays),) + arrays[0].shape, jnp.float32),
        in_specs=[vmem] * len(arrays),
        out_specs=vmem,
    )(*arrays)


def make_coefs(raw_ref, coef_ref, lay):
    lane = lax.broadcasted_iota(jnp.int32, (TILE, raw_ref.shape[-1]), 1)
    last = raw_ref.shape[-1] - 1

    def from_below(value):
        return jnp.where(lane == 0, 0.0, pltpu.roll(value, 1, 1))

    def from_above(value):
        return jnp.where(lane == last, 0.0, pltpu.roll(value, last, 1))

    def one_row(row, unused):
        for tile in range(lay.span // TILE):
            lines = slice(TILE * tile, TILE * tile + TILE)
            n_x, n_y = raw_ref[0, row, lines, :], raw_ref[1, row, lines, :]
            xx, yy = n_x * n_x, n_y * n_y
            flat = xx + yy
            zz = 1.0 - flat
            half = 0.5 * jnp.sqrt(zz)
            xz, yz = half * n_x, half * n_y
            values = (
                xx, 1.0 - xx, yy, 1.0 - yy, 0.5 * n_x * n_y,
                from_below(zz), from_below(flat), from_below(xz), from_below(yz),
                from_above(zz), from_above(flat), from_above(xz), from_above(yz),
            )
            for i, value in enumerate(values):
                coef_ref[i, row, lines, :] = value
        return unused

    lax.fori_loop(0, lay.width, one_row, 0)


def run_steps(state, coef_ref, source, inject_ref, image_ref, lay):
    z_count = state.shape[-1]
    last = z_count - 1
    lane = lax.broadcasted_iota(jnp.int32, (TILE, z_count), 1)
    chunk = next(size for size in (8, 4, 2, 1) if lay.width % size == 0)

    def row_of(now, field, row, tile):
        base = TILE + TILE * tile
        middle = state[now, field, row, base : base + TILE, :]
        low = state[now, field, row, base - 1 : base - 1 + TILE, :]
        high = state[now, field, row, base + 1 : base + 1 + TILE, :]
        return middle, high - low, high + low

    def sweep(step, now, new, first, tile, wave):
        turn = lax.rem(REC_Z - step + z_count, z_count)
        lines = slice(TILE * tile, TILE * tile + TILE)
        inner = slice(TILE + TILE * tile, 2 * TILE + TILE * tile)
        pair = (2 * wave, 2 * wave + 1)
        before = [row_of(now, field, first, tile) for field in pair]
        here = [row_of(now, field, first + 1, tile) for field in pair]
        for i in range(chunk):
            row = first + i
            beyond = [row_of(now, field, row + 2, tile) for field in pair]
            coef = [coef_ref[n, row, lines, :] for n in range(COEFS)]
            xx, xx0, yy, yy0, xy = coef[:5]
            zz_b, zz0_b, xz_b, yz_b, zz_a, zz0_a, xz_a, yz_a = coef[5:13]
            velocity, axial_gain, cross_gain = coef[13:]

            def terms(field):
                f, diff_y, sum_y = here[field]
                sum_x = beyond[field][0] + before[field][0]
                diff_x = beyond[field][0] - before[field][0]
                mixed = beyond[field][1] - before[field][1]
                below = xz_b * diff_x + yz_b * diff_y
                above = xz_a * diff_x + yz_a * diff_y
                return f, sum_x, sum_y, xy * mixed, below, above

            p, sum_x, sum_y, mixed, below, above = terms(0)
            across = xx0 * sum_x + yy0 * sum_y - mixed
            across += pltpu.roll(zz0_b * p - below, last, 1) + pltpu.roll(zz0_a * p + above, 1, 1)
            twice_p = p + p
            across -= twice_p + twice_p
            q, sum_x, sum_y, mixed, below, above = terms(1)
            axial = xx * sum_x + yy * sum_y + mixed
            axial += pltpu.roll(zz_b * q + below, last, 1) + pltpu.roll(zz_a * q - above, 1, 1)
            twice_q = q + q
            axial -= twice_q
            old_p = state[new, pair[0], row + 1, inner, :]
            old_q = state[new, pair[1], row + 1, inner, :]
            new_p = (twice_p - old_p) + (axial_gain * across + cross_gain * axial)
            new_q = (twice_q - old_q) + (cross_gain * across + velocity * axial)
            if wave == 1:
                pulse = pltpu.roll(inject_ref[row, lines, :], turn, 1)
                pulse = velocity * jnp.where(lane == REC_Z, pulse, 0.0)
                new_p, new_q = new_p + pulse, new_q + pulse
            state[new, pair[0], row + 1, inner, :] = new_p
            state[new, pair[1], row + 1, inner, :] = new_q
            if wave == 1:
                image_ref[row, lines, :] += state[new, 0, row + 1, inner, :] * new_p
            before, here = here, beyond

    def one_step(step, now):
        def sweeps(wave):
            def one_chunk(first):
                for tile in range(lay.span // TILE):
                    sweep(step, now, 1 - now, first, tile, wave)

            if chunk == lay.width:
                one_chunk(0)
            else:
                lax.fori_loop(0, lay.width // chunk, lambda n, u: (one_chunk(n * chunk), u)[1], 0)

        sweeps(0)
        source_x, first, source_ref = source
        first = pl.multiple_of(first, TILE)
        pulse = coef_ref[COEFS - 3, source_x, pl.ds(first, TILE), :] * source_ref[step]
        for field in (0, 1):
            state[1 - now, field, source_x + 1, pl.ds(TILE + first, TILE), :] += pulse
        sweeps(1)

    def two_steps(i, unused):
        one_step(2 * i, 0)
        one_step(2 * i + 1, 1)
        return unused

    lax.fori_loop(0, lay.steps // 2, two_steps, 0)
    if lay.steps % 2:
        one_step(lay.steps - 1, 0)


def clear_edges(state, lay):
    rows, lines = state.shape[2], state.shape[3]
    edge = jnp.zeros((lines,) + state.shape[4:], jnp.float32)
    strip = jnp.zeros((rows, TILE) + state.shape[4:], jnp.float32)
    for time in range(state.shape[0]):
        for field in range(state.shape[1]):
            state[time, field, 0] = edge
            state[time, field, rows - 1] = edge
            state[time, field, :, :TILE] = strip
            state[time, field, :, lines - TILE :] = strip


def wave_kernel(lay, scalars, source_ref, receiver_ref, *refs):
    waves_own, waves_other, model_own, model_other, pieces = (
        refs[i * lay.domain : (i + 1) * lay.domain] for i in range(5)
    )
    raw, coef_ref, image_ref, state = refs[5 * lay.domain :]
    clear_edges(state, lay)

    def store_wave(row, ref):
        for i in range(8):
            time, field = (i >> 1) & 1, 2 * (i >> 2) + (i & 1)
            state[time, field, row + 1, TILE : TILE + lay.span, :] = ref[i]

    def store_model(row, ref):
        for i in range(5):
            target = coef_ref.at[COEFS - 3 + i, row] if i < 3 else raw.at[i - 3, row]
            target[...] = ref[i]

    gather_rows(lay, waves_own, waves_other, store_wave)
    gather_rows(lay, model_own, model_other, store_model)
    make_coefs(raw, coef_ref, lay)
    image_ref[...] = jnp.zeros_like(image_ref)
    run_steps(state, coef_ref, (scalars[0], scalars[1], source_ref), receiver_ref, image_ref, lay)
    kc, c, d, unused = lay.position()
    skip = (2 * kc + c) * lay.own - (lay.start(kc) + lay.shift(c) - lay.pad[0])
    if lay.own % TILE == 0:
        skip = pl.multiple_of(skip, TILE)
    for r, piece in enumerate(pieces):
        first = lax.rem(d + r, lay.domain) * lay.rows
        for row in range(lay.rows):
            if lay.own % TILE == 0:
                piece[row] = image_ref[first + row, pl.ds(skip, lay.own), :]
            else:
                piece[row] = pltpu.roll(image_ref[first + row], lay.span - skip, 0)[: lay.own]


def frame_kernel(lay, scalars, owners, *refs, slab):
    pieces, outs, frame = refs[: lay.domain], refs[lay.domain : -1], refs[-1]
    unused, c, d, unused = lay.position()
    frame[...] = jnp.zeros_like(frame)
    room = -(-lay.own // TILE) * TILE + TILE
    filler = jnp.zeros((room - lay.own, frame.shape[-1]), jnp.float32)
    for r, piece in enumerate(pieces):
        source = lax.rem(d - r + lay.domain, lay.domain)
        place = scalars[2 + source // lay.half] + (2 * lax.rem(source, lay.half) + c) * lay.own
        first = pl.multiple_of(place & ~(TILE - 1), TILE)
        for row in range(lay.rows):
            moved = pltpu.roll(jnp.concatenate([piece[row], filler]), place & (TILE - 1), 0)
            frame[row, pl.ds(first, room), :] += moved
    for r, out in enumerate(outs):
        first = pl.multiple_of(owners[lax.axis_index("shot") ^ r] * slab, TILE)
        for row in range(lay.rows):
            out[row] = frame[row, pl.ds(first, slab), :]


def call(kernel, cost, lay, outs, scratch, scalars, *operands):
    smem = pl.BlockSpec(memory_space=pltpu.SMEM)
    vmem = pl.BlockSpec(memory_space=pltpu.VMEM)
    held = sum(4 * math.prod(array.shape) for array in [*operands, *outs, *scratch])
    return pl.pallas_call(
        functools.partial(kernel, lay),
        out_shape=outs,
        in_specs=[smem] * len(scalars) + [vmem] * len(operands),
        out_specs=[vmem] * len(outs),
        scratch_shapes=scratch,
        compiler_params=pltpu.CompilerParams(vmem_limit_bytes=held + held // 8 + 2**21),
        cost_estimate=pl.CostEstimate(flops=0, bytes_accessed=cost, transcendentals=0),
    )(*scalars, *operands)


def per_device(
    velocity,
    thomsen_eps,
    thomsen_delta,
    tilt_angle,
    azimuth,
    shot_anchor,
    source_x,
    source_y,
    wavelet,
    receiver_x,
    receiver_y,
    traces,
    source_now,
    source_before,
    receiver_now,
    receiver_before,
    slab_owner,
):
    rows, lines, z_count = source_now.shape[2:]
    steps = wavelet.shape[1]
    domain, shots = lax.axis_size("domain"), lax.axis_size("shot")
    lay = Layout(domain, shots, rows, lines, steps)
    d, s = lax.axis_index("domain"), lax.axis_index("shot")
    zero = jnp.int32(0)

    tight = lay.pad == (0, 0)

    def wave_messages(fields):
        fields = [jnp.pad(field[0], ((0, 0), (0, 0), lay.pad, (0, 0))) for field in fields]
        messages = []
        for r in range(domain):
            k = lax.rem(d + r, domain)
            spot = (zero, (k & 1) * lay.part, lay.start(k >> 1), zero)
            size = (2, lay.part, lay.chip, z_count)
            messages.append(jnp.concatenate([lax.dynamic_slice(field, spot, size) for field in fields]))
        return messages

    def send(messages):
        return [lax.ppermute(messages[r], ("domain", "shot"), pairs) for r, pairs in lay.rounds()]

    def other_core(messages):
        return [swapped(message, "shot", 1) for message in messages]

    messages = wave_messages((source_now, source_before, receiver_now, receiver_before))
    velocity, messages[0] = lax.optimization_barrier((velocity, messages[0]))
    waves = send(messages)
    model = medium(velocity, thomsen_eps, thomsen_delta, tilt_angle, azimuth)
    slab = model.shape[2]
    whole = jnp.zeros(model.shape[:2] + (shots * slab, z_count), jnp.float32)
    for r in range(shots):
        block = swapped(model, "shot", r) if r else model
        whole = lax.dynamic_update_slice(whole, block, (zero, zero, (s ^ r) * slab, zero))
    model = whole
    anchor = shot_anchor[0]
    if tight:
        first_line = anchor
    else:
        model = lax.dynamic_slice_in_dim(model, anchor, lines, 2)
        model = jnp.pad(model, ((0, 0), (0, 0), lay.pad, (0, 0)))
        first_line = zero
    messages = []
    for r in range(domain):
        k = lax.rem(d + r, domain)
        spot = (zero, (k & 1) * lay.part, first_line + lay.start(k >> 1), zero)
        messages.append(lax.dynamic_slice(model, spot, (5, lay.part, lay.chip, z_count)))
    *messages, waves[-1] = lax.optimization_barrier((*messages, waves[-1]))
    models = send(messages)
    *waves, models[0] = lax.optimization_barrier((*waves, models[0]))
    waves_other, models_other = other_core(waves), other_core(models)

    traces, waves[0] = lax.optimization_barrier((traces, waves[0]))
    table = table_of(traces, wavelet, receiver_x, receiver_y, source_x, source_y, shot_anchor)
    receiver_pulse, source_pulse, scalars = pulses(lay, table, swapped(table, "shot", 1), z_count)
    block = (lay.width, lay.span, z_count)
    pieces = call(
        wave_kernel,
        60_000_000,
        lay,
        [jax.ShapeDtypeStruct((rows, lay.own, z_count), jnp.float32)] * domain,
        [
            pltpu.VMEM((2,) + block, jnp.float32),
            pltpu.VMEM((COEFS,) + block, jnp.float32),
            pltpu.VMEM(block, jnp.float32),
            pltpu.VMEM((2, 4, lay.width + 2, lay.span + 2 * TILE, z_count), jnp.float32),
        ],
        (scalars,),
        source_pulse,
        receiver_pulse,
        *waves,
        *waves_other,
        *models,
        *models_other,
    )

    pieces = [
        swapped_round(piece, "domain", r) if r else piece for r, piece in enumerate(pieces)
    ]
    room = -(-lay.own // TILE) * TILE + TILE
    parts = call(
        functools.partial(frame_kernel, slab=slab),
        2_000_000,
        lay,
        [jax.ShapeDtypeStruct((rows, slab, z_count), jnp.float32)] * shots,
        [pltpu.VMEM((rows, shots * slab + room, z_count), jnp.float32)],
        (scalars, slab_owner),
        *pieces,
    )
    total = parts[0]
    for r in range(1, shots):
        total = total + swapped(parts[r], "shot", r)
    return total / steps


def solution(mesh):
    in_specs = (
        P(("groups", "domain"), "shot", None),
        P(("groups", "domain"), "shot", None),
        P(("groups", "domain"), "shot", None),
        P(("groups", "domain"), "shot", None),
        P(("groups", "domain"), "shot", None),
        P(("groups", "shot")),
        P(("groups", "shot")),
        P(("groups", "shot")),
        P(("groups", "shot"), None),
        P(("groups", "shot"), None),
        P(("groups", "shot"), None),
        P(("groups", "shot"), None, None),
        P(("groups", "shot"), None, "domain", None, None),
        P(("groups", "shot"), None, "domain", None, None),
        P(("groups", "shot"), None, "domain", None, None),
        P(("groups", "shot"), None, "domain", None, None),
        P("groups"),
    )
    out_specs = P(("groups", "domain"), "shot", None)
    return jax.shard_map(
        per_device, mesh=mesh, in_specs=in_specs, out_specs=out_specs, check_vma=False
    )
```

```python
import functools
import math

import jax
import jax.numpy as jnp
from jax import lax
from jax.experimental import pallas as pl
from jax.experimental.pallas import tpu as pltpu
from jax.sharding import PartitionSpec as P

SRC_Z = 3
REC_Z = 1
TILE = 8
COEFS = 16


class Layout:
    def __init__(self, domain, shots, rows, lines, steps):
        self.domain, self.shots, self.rows, self.lines, self.steps = domain, shots, rows, lines, steps
        self.half = domain // 2
        self.width = rows * domain
        self.own = lines // domain
        halo = -(-steps // TILE) * TILE
        if self.half == 2 and self.own % TILE == 0:
            self.pad = (0, 0)
            self.chip = 2 * self.own + halo
            self.stride = lines - self.chip
            self.span = self.own + 2 * halo
        else:
            self.chip = -(-(2 * self.own + 2 * halo) // TILE) * TILE
            self.pad = (halo, max(0, (self.half - 1) * 2 * self.own + self.chip - halo - lines))
            self.stride = 2 * self.own
            self.span = self.chip

    def start(self, kc):
        return kc * self.stride

    def shift(self, c):
        return c * (self.chip - self.span)

    def position(self):
        d, s = lax.axis_index("domain"), lax.axis_index("shot")
        return lax.rem(d, self.half), s & 1, d, d // self.half

    def chip_of(self, d, r):
        return lax.rem((d >> 1) + r, self.half) if not isinstance(d, int) else ((d >> 1) + r) % self.half

    def rounds(self):
        count = self.domain * self.shots
        for r in range(self.half):
            pairs = []
            for d in range(self.domain):
                for s in range(self.shots):
                    to_d = self.half * (s & 1) + self.chip_of(d, r)
                    to_s = (s & ~1) | (d & 1)
                    pairs.append((d * self.shots + s, to_d * self.shots + to_s))
            assert len({pair[1] for pair in pairs}) == count
            yield r, pairs


def swapped(value, axis, bit):
    count = lax.axis_size(axis)
    return lax.ppermute(value, axis, [(i, i ^ bit) for i in range(count)])


def tied(value, *others):
    return lax.optimization_barrier((value, *others))[0]


def swapped_round(value, axis, r):
    count = lax.axis_size(axis)
    return lax.ppermute(value, axis, [(i, (i + r) % count) for i in range(count)])


def gather_rows(lay, own_refs, other_refs, store):
    kc, c, unused, unused = lay.position()
    window = pl.ds(pl.multiple_of(lay.shift(c), TILE), lay.span)
    for core, refs in ((c, own_refs), (1 - c, other_refs)):
        for r, ref in enumerate(refs):
            source = 2 * lax.rem(kc - r + lay.half, lay.half) + core
            for part in range(lay.rows):
                store(source * lay.rows + part, ref.at[:, part, window, :])


def table_kernel(traces, wavelet, rec_x, rec_y, src_x, src_y, anchor, table):
    steps = traces.shape[1]
    table[...] = jnp.zeros_like(table)
    table[:steps] = traces[0]
    table[steps : steps + 1, :steps] = wavelet[...]
    row = (1, table.shape[1])
    table[steps + 1 : steps + 2] = rec_x[...].astype(jnp.float32)
    table[steps + 2 : steps + 3] = rec_y[...].astype(jnp.float32)
    for i, scalar in enumerate((src_x, src_y, anchor)):
        table[steps + 3 + i : steps + 4 + i] = jnp.full(row, scalar[0], jnp.int32).astype(jnp.float32)


def table_of(*arrays):
    steps, receivers = arrays[0].shape[1:]
    smem, vmem = (pl.BlockSpec(memory_space=space) for space in (pltpu.SMEM, pltpu.VMEM))
    return pl.pallas_call(
        table_kernel,
        out_shape=jax.ShapeDtypeStruct((-(-(steps + 6) // TILE) * TILE, receivers), jnp.float32),
        in_specs=[vmem] * 4 + [smem] * 3,
        out_specs=vmem,
        compiler_params=pltpu.CompilerParams(vmem_limit_bytes=2**21),
    )(*arrays)


def pulse_kernel(lay, mine, twin, receiver_out, source_out, scalars, padded):
    kc, c, d, works_on = lay.position()
    steps, lanes = lay.steps, receiver_out.shape[-1]
    window = lay.start(kc) + lay.shift(c) - lay.pad[0]
    table = jnp.where(works_on == c, mine[...], twin[...])

    def scalar(values, row):
        return jnp.max(values[row : row + 1]).astype(jnp.int32)

    src_x, src_y = scalar(table, steps + 3), scalar(table, steps + 4) - window
    first = jnp.clip(src_y, 0, lay.span - 1) & ~(TILE - 1)
    anchors = scalar(mine[...], steps + 5), scalar(twin[...], steps + 5)
    scalars[0], scalars[1] = src_x, first
    scalars[2] = jnp.where(c == 0, anchors[0], anchors[1])
    scalars[3] = jnp.where(c == 0, anchors[1], anchors[0])

    lane = lax.broadcasted_iota(jnp.int32, (TILE, lanes), 1)
    line = lax.broadcasted_iota(jnp.int32, (TILE, lanes), 0)
    spot = (lane == SRC_Z) & (line + first == src_y)
    at_step = lax.broadcasted_iota(jnp.int32, (1, table.shape[1]), 1)
    for step in range(steps):
        amount = jnp.sum(jnp.where(at_step == step, table[steps : steps + 1], 0.0))
        source_out[step] = jnp.where(spot, amount, 0.0)

    lines = lax.broadcasted_iota(jnp.int32, (lay.span, table.shape[1]), 0) + window
    there = (lines == table[steps + 2 : steps + 3].astype(jnp.int32)).astype(jnp.float32)
    padded[...] = jnp.zeros_like(padded)

    def one_row(row, unused):
        here = table[steps + 1 : steps + 2].astype(jnp.int32) == row
        padded[:steps] = jnp.where(here, table[:steps], 0.0)
        receiver_out[row] = lax.dot_general(
            there,
            padded[...],
            (((1,), (1,)), ((), ())),
            precision=lax.Precision.HIGHEST,
            preferred_element_type=jnp.float32,
        )
        return unused

    lax.fori_loop(0, lay.width, one_row, 0)


def pulses(lay, mine, twin, z_count):
    shapes = [(lay.width, lay.span, z_count), (lay.steps, TILE, z_count)]
    held = 4 * (2 * math.prod(shapes[0]) + z_count * mine.shape[1])
    smem, vmem = (pl.BlockSpec(memory_space=space) for space in (pltpu.SMEM, pltpu.VMEM))
    return pl.pallas_call(
        functools.partial(pulse_kernel, lay),
        out_shape=[jax.ShapeDtypeStruct(shape, jnp.float32) for shape in shapes]
        + [jax.ShapeDtypeStruct((4,), jnp.int32)],
        in_specs=[vmem] * 2,
        out_specs=[vmem, vmem, smem],
        scratch_shapes=[pltpu.VMEM((z_count, mine.shape[1]), jnp.float32)],
        compiler_params=pltpu.CompilerParams(vmem_limit_bytes=held + 2**21),
    )(mine, twin)


def sin_cos(angle):
    square = angle * angle
    sine, cosine = 1.0 / 6227020800.0, -1.0 / 87178291200.0
    for n in (11, 9, 7, 5, 3, 1):
        sine = sine * square + (-1.0) ** (n // 2) / math.factorial(n)
    for n in (12, 10, 8, 6, 4, 2, 0):
        cosine = cosine * square + (-1.0) ** (n // 2) / math.factorial(n)
    return sine * angle, cosine


def medium_kernel(velocity, eps, delta, tilt, azimuth, out):
    speed = velocity[...]
    out[0] = speed
    out[1] = speed * (1.0 + 2.0 * eps[...])
    out[2] = speed * jnp.sqrt(1.0 + 2.0 * delta[...])
    sin_tilt, unused = sin_cos(tilt[...])
    sine, cosine = sin_cos(0.5 * azimuth[...])
    out[3] = sin_tilt * (1.0 - 2.0 * sine * sine)
    out[4] = sin_tilt * (2.0 * sine * cosine)


def medium(*arrays):
    vmem = pl.BlockSpec(memory_space=pltpu.VMEM)
    return pl.pallas_call(
        medium_kernel,
        out_shape=jax.ShapeDtypeStruct((len(arrays),) + arrays[0].shape, jnp.float32),
        in_specs=[vmem] * len(arrays),
        out_specs=vmem,
    )(*arrays)


def make_coefs(raw_ref, coef_ref, lay):
    lane = lax.broadcasted_iota(jnp.int32, (TILE, raw_ref.shape[-1]), 1)
    last = raw_ref.shape[-1] - 1

    def from_below(value):
        return jnp.where(lane == 0, 0.0, pltpu.roll(value, 1, 1))

    def from_above(value):
        return jnp.where(lane == last, 0.0, pltpu.roll(value, last, 1))

    def one_row(row, unused):
        for tile in range(lay.span // TILE):
            lines = slice(TILE * tile, TILE * tile + TILE)
            n_x, n_y = raw_ref[0, row, lines, :], raw_ref[1, row, lines, :]
            xx, yy = n_x * n_x, n_y * n_y
            flat = xx + yy
            zz = 1.0 - flat
            half = 0.5 * jnp.sqrt(zz)
            xz, yz = half * n_x, half * n_y
            values = (
                xx, 1.0 - xx, yy, 1.0 - yy, 0.5 * n_x * n_y,
                from_below(zz), from_below(flat), from_below(xz), from_below(yz),
                from_above(zz), from_above(flat), from_above(xz), from_above(yz),
            )
            for i, value in enumerate(values):
                coef_ref[i, row, lines, :] = value
        return unused

    lax.fori_loop(0, lay.width, one_row, 0)


def run_steps(state, coef_ref, source, inject_ref, image_ref, lay):
    z_count = state.shape[-1]
    last = z_count - 1
    lane = lax.broadcasted_iota(jnp.int32, (TILE, z_count), 1)
    chunk = next(size for size in (8, 4, 2, 1) if lay.width % size == 0)

    def row_of(now, field, row, tile):
        base = TILE + TILE * tile
        middle = state[now, field, row, base : base + TILE, :]
        low = state[now, field, row, base - 1 : base - 1 + TILE, :]
        high = state[now, field, row, base + 1 : base + 1 + TILE, :]
        return middle, high - low, high + low

    def sweep(step, now, new, first, tile, wave):
        turn = lax.rem(REC_Z - step + z_count, z_count)
        lines = slice(TILE * tile, TILE * tile + TILE)
        inner = slice(TILE + TILE * tile, 2 * TILE + TILE * tile)
        pair = (2 * wave, 2 * wave + 1)
        before = [row_of(now, field, first, tile) for field in pair]
        here = [row_of(now, field, first + 1, tile) for field in pair]
        for i in range(chunk):
            row = first + i
            beyond = [row_of(now, field, row + 2, tile) for field in pair]
            coef = [coef_ref[n, row, lines, :] for n in range(COEFS)]
            xx, xx0, yy, yy0, xy = coef[:5]
            zz_b, zz0_b, xz_b, yz_b, zz_a, zz0_a, xz_a, yz_a = coef[5:13]
            velocity, axial_gain, cross_gain = coef[13:]

            def terms(field):
                f, diff_y, sum_y = here[field]
                sum_x = beyond[field][0] + before[field][0]
                diff_x = beyond[field][0] - before[field][0]
                mixed = beyond[field][1] - before[field][1]
                below = xz_b * diff_x + yz_b * diff_y
                above = xz_a * diff_x + yz_a * diff_y
                return f, sum_x, sum_y, xy * mixed, below, above

            p, sum_x, sum_y, mixed, below, above = terms(0)
            across = xx0 * sum_x + yy0 * sum_y - mixed
            across += pltpu.roll(zz0_b * p - below, last, 1) + pltpu.roll(zz0_a * p + above, 1, 1)
            twice_p = p + p
            across -= twice_p + twice_p
            q, sum_x, sum_y, mixed, below, above = terms(1)
            axial = xx * sum_x + yy * sum_y + mixed
            axial += pltpu.roll(zz_b * q + below, last, 1) + pltpu.roll(zz_a * q - above, 1, 1)
            twice_q = q + q
            axial -= twice_q
            old_p = state[new, pair[0], row + 1, inner, :]
            old_q = state[new, pair[1], row + 1, inner, :]
            new_p = (twice_p - old_p) + (axial_gain * across + cross_gain * axial)
            new_q = (twice_q - old_q) + (cross_gain * across + velocity * axial)
            if wave == 1:
                pulse = pltpu.roll(inject_ref[row, lines, :], turn, 1)
                pulse = velocity * jnp.where(lane == REC_Z, pulse, 0.0)
                new_p, new_q = new_p + pulse, new_q + pulse
            state[new, pair[0], row + 1, inner, :] = new_p
            state[new, pair[1], row + 1, inner, :] = new_q
            if wave == 1:
                image_ref[row, lines, :] += state[new, 0, row + 1, inner, :] * new_p
            before, here = here, beyond

    def one_step(step, now):
        def sweeps(wave):
            def one_chunk(first):
                for tile in range(lay.span // TILE):
                    sweep(step, now, 1 - now, first, tile, wave)

            if chunk == lay.width:
                one_chunk(0)
            else:
                lax.fori_loop(0, lay.width // chunk, lambda n, u: (one_chunk(n * chunk), u)[1], 0)

        sweeps(0)
        source_x, first, source_ref = source
        first = pl.multiple_of(first, TILE)
        pulse = coef_ref[COEFS - 3, source_x, pl.ds(first, TILE), :] * source_ref[step]
        for field in (0, 1):
            state[1 - now, field, source_x + 1, pl.ds(TILE + first, TILE), :] += pulse
        sweeps(1)

    def two_steps(i, unused):
        one_step(2 * i, 0)
        one_step(2 * i + 1, 1)
        return unused

    lax.fori_loop(0, lay.steps // 2, two_steps, 0)
    if lay.steps % 2:
        one_step(lay.steps - 1, 0)


def clear_edges(state, lay):
    rows, lines = state.shape[2], state.shape[3]
    edge = jnp.zeros((lines,) + state.shape[4:], jnp.float32)
    strip = jnp.zeros((rows, TILE) + state.shape[4:], jnp.float32)
    for time in range(state.shape[0]):
        for field in range(state.shape[1]):
            state[time, field, 0] = edge
            state[time, field, rows - 1] = edge
            state[time, field, :, :TILE] = strip
            state[time, field, :, lines - TILE :] = strip


def wave_kernel(lay, scalars, source_ref, receiver_ref, *refs):
    waves_own, waves_other, model_own, model_other = (refs[i * lay.half : (i + 1) * lay.half] for i in range(4))
    pieces, (raw, coef_ref, image_ref, state) = refs[4 * lay.half : -4], refs[-4:]
    clear_edges(state, lay)

    def store_wave(row, ref):
        for i in range(8):
            time, field = (i >> 1) & 1, 2 * (i >> 2) + (i & 1)
            state[time, field, row + 1, TILE : TILE + lay.span, :] = ref[i]

    def store_model(row, ref):
        for i in range(5):
            target = coef_ref.at[COEFS - 3 + i, row] if i < 3 else raw.at[i - 3, row]
            target[...] = ref[i]

    gather_rows(lay, waves_own, waves_other, store_wave)
    gather_rows(lay, model_own, model_other, store_model)
    make_coefs(raw, coef_ref, lay)
    image_ref[...] = jnp.zeros_like(image_ref)
    run_steps(state, coef_ref, (scalars[0], scalars[1], source_ref), receiver_ref, image_ref, lay)
    kc, c, d, unused = lay.position()
    skip = (2 * kc + c) * lay.own - (lay.start(kc) + lay.shift(c) - lay.pad[0])
    if lay.own % TILE == 0:
        skip = pl.multiple_of(skip, TILE)
    for r, piece in enumerate(pieces):
        first = lax.rem(d + r, lay.domain) * lay.rows
        for row in range(lay.rows):
            if lay.own % TILE == 0:
                piece[row] = image_ref[first + row, pl.ds(skip, lay.own), :]
            else:
                piece[row] = pltpu.roll(image_ref[first + row], lay.span - skip, 0)[: lay.own]


def frame_kernel(lay, scalars, owners, *refs, slab):
    pieces, outs, frame = refs[: lay.domain], refs[lay.domain : -1], refs[-1]
    unused, c, d, unused = lay.position()
    frame[...] = jnp.zeros_like(frame)
    room = -(-lay.own // TILE) * TILE + TILE
    filler = jnp.zeros((room - lay.own, frame.shape[-1]), jnp.float32)
    for r, piece in enumerate(pieces):
        source = lax.rem(d - r + lay.domain, lay.domain)
        place = scalars[2 + source // lay.half] + (2 * lax.rem(source, lay.half) + c) * lay.own
        first = pl.multiple_of(place & ~(TILE - 1), TILE)
        for row in range(lay.rows):
            moved = pltpu.roll(jnp.concatenate([piece[row], filler]), place & (TILE - 1), 0)
            frame[row, pl.ds(first, room), :] += moved
    for r, out in enumerate(outs):
        first = pl.multiple_of(owners[lax.axis_index("shot") ^ r] * slab, TILE)
        for row in range(lay.rows):
            out[row] = frame[row, pl.ds(first, slab), :]


def call(kernel, cost, lay, outs, scratch, scalars, *operands):
    smem = pl.BlockSpec(memory_space=pltpu.SMEM)
    vmem = pl.BlockSpec(memory_space=pltpu.VMEM)
    held = sum(4 * math.prod(array.shape) for array in [*operands, *outs, *scratch])
    return pl.pallas_call(
        functools.partial(kernel, lay),
        out_shape=outs,
        in_specs=[smem] * len(scalars) + [vmem] * len(operands),
        out_specs=[vmem] * len(outs),
        scratch_shapes=scratch,
        compiler_params=pltpu.CompilerParams(vmem_limit_bytes=held + held // 8 + 2**21),
        cost_estimate=pl.CostEstimate(flops=0, bytes_accessed=cost, transcendentals=0),
    )(*scalars, *operands)


def per_device(
    velocity,
    thomsen_eps,
    thomsen_delta,
    tilt_angle,
    azimuth,
    shot_anchor,
    source_x,
    source_y,
    wavelet,
    receiver_x,
    receiver_y,
    traces,
    source_now,
    source_before,
    receiver_now,
    receiver_before,
    slab_owner,
):
    rows, lines, z_count = source_now.shape[2:]
    steps = wavelet.shape[1]
    domain, shots = lax.axis_size("domain"), lax.axis_size("shot")
    lay = Layout(domain, shots, rows, lines, steps)
    d, s = lax.axis_index("domain"), lax.axis_index("shot")
    zero = jnp.int32(0)

    tight = lay.pad == (0, 0)

    def wave_messages(fields):
        fields = [jnp.pad(field[0], ((0, 0), (0, 0), lay.pad, (0, 0))) for field in fields]
        messages = []
        for r in range(lay.half):
            first = lay.start(lay.chip_of(d, r))
            messages.append(
                jnp.concatenate([lax.dynamic_slice_in_dim(field, first, lay.chip, 2) for field in fields])
            )
        return messages

    def send(messages):
        return [lax.ppermute(messages[r], ("domain", "shot"), pairs) for r, pairs in lay.rounds()]

    def other_core(messages):
        return [swapped(message, "shot", 1) for message in messages]

    messages = wave_messages((source_now, source_before, receiver_now, receiver_before))
    waves = send(messages)
    model = medium(velocity, thomsen_eps, thomsen_delta, tilt_angle, azimuth)
    slab = model.shape[2]
    whole = jnp.zeros(model.shape[:2] + (shots * slab, z_count), jnp.float32)
    for r in range(shots):
        block = swapped(model, "shot", r) if r else model
        whole = lax.dynamic_update_slice(whole, block, (zero, zero, (s ^ r) * slab, zero))
    model = whole
    anchor = shot_anchor[0]
    if tight:
        first_line = anchor
    else:
        model = lax.dynamic_slice_in_dim(model, anchor, lines, 2)
        model = jnp.pad(model, ((0, 0), (0, 0), lay.pad, (0, 0)))
        first_line = zero
    messages = []
    for r in range(lay.half):
        first = first_line + lay.start(lay.chip_of(d, r))
        messages.append(lax.dynamic_slice_in_dim(model, first, lay.chip, 2))
    models = send(messages)
    *waves, models[0] = lax.optimization_barrier((*waves, models[0]))
    waves_other = other_core(waves)

    traces, waves[0] = lax.optimization_barrier((traces, waves[0]))
    table = table_of(traces, wavelet, receiver_x, receiver_y, source_x, source_y, shot_anchor)
    receiver_pulse, source_pulse, scalars = pulses(lay, table, swapped(table, "shot", 1), z_count)
    *models, receiver_pulse = lax.optimization_barrier((*models, receiver_pulse))
    models_other = other_core(models)
    block = (lay.width, lay.span, z_count)
    pieces = call(
        wave_kernel,
        60_000_000,
        lay,
        [jax.ShapeDtypeStruct((rows, lay.own, z_count), jnp.float32)] * domain,
        [
            pltpu.VMEM((2,) + block, jnp.float32),
            pltpu.VMEM((COEFS,) + block, jnp.float32),
            pltpu.VMEM(block, jnp.float32),
            pltpu.VMEM((2, 4, lay.width + 2, lay.span + 2 * TILE, z_count), jnp.float32),
        ],
        (scalars,),
        source_pulse,
        receiver_pulse,
        *waves,
        *waves_other,
        *models,
        *models_other,
    )

    pieces = [
        swapped_round(piece, "domain", r) if r else piece for r, piece in enumerate(pieces)
    ]
    room = -(-lay.own // TILE) * TILE + TILE
    parts = call(
        functools.partial(frame_kernel, slab=slab),
        2_000_000,
        lay,
        [jax.ShapeDtypeStruct((rows, slab, z_count), jnp.float32)] * shots,
        [pltpu.VMEM((rows, shots * slab + room, z_count), jnp.float32)],
        (scalars, slab_owner),
        *pieces,
    )
    total = parts[0]
    for r in range(1, shots):
        total = total + swapped(parts[r], "shot", r)
    return total / steps


def solution(mesh):
    in_specs = (
        P(("groups", "domain"), "shot", None),
        P(("groups", "domain"), "shot", None),
        P(("groups", "domain"), "shot", None),
        P(("groups", "domain"), "shot", None),
        P(("groups", "domain"), "shot", None),
        P(("groups", "shot")),
        P(("groups", "shot")),
        P(("groups", "shot")),
        P(("groups", "shot"), None),
        P(("groups", "shot"), None),
        P(("groups", "shot"), None),
        P(("groups", "shot"), None, None),
        P(("groups", "shot"), None, "domain", None, None),
        P(("groups", "shot"), None, "domain", None, None),
        P(("groups", "shot"), None, "domain", None, None),
        P(("groups", "shot"), None, "domain", None, None),
        P("groups"),
    )
    out_specs = P(("groups", "domain"), "shot", None)
    return jax.shard_map(
        per_device, mesh=mesh, in_specs=in_specs, out_specs=out_specs, check_vma=False
    )
```

```python
import functools
import math

import jax
import jax.numpy as jnp
from jax import lax
from jax.experimental import pallas as pl
from jax.experimental.pallas import tpu as pltpu
from jax.sharding import PartitionSpec as P

SRC_Z = 3
REC_Z = 1
TILE = 8
COEFS = 16


class Layout:
    def __init__(self, domain, shots, rows, lines, steps):
        self.domain, self.shots, self.rows, self.lines, self.steps = domain, shots, rows, lines, steps
        self.half = domain // 2
        self.width = rows * domain
        self.own = lines // domain
        halo = -(-steps // TILE) * TILE
        if self.half == 2 and self.own % TILE == 0:
            self.pad = (0, 0)
            self.chip = 2 * self.own + halo
            self.stride = lines - self.chip
            self.span = self.own + 2 * halo
        else:
            self.chip = -(-(2 * self.own + 2 * halo) // TILE) * TILE
            self.pad = (halo, max(0, (self.half - 1) * 2 * self.own + self.chip - halo - lines))
            self.stride = 2 * self.own
            self.span = self.chip

    def start(self, kc):
        return kc * self.stride

    def shift(self, c):
        return c * (self.chip - self.span)

    def position(self):
        d, s = lax.axis_index("domain"), lax.axis_index("shot")
        return lax.rem(d, self.half), s & 1, d, d // self.half

    def chip_of(self, d, r):
        return lax.rem((d >> 1) + r, self.half) if not isinstance(d, int) else ((d >> 1) + r) % self.half

    def rounds(self):
        count = self.domain * self.shots
        for r in range(self.half):
            pairs = []
            for d in range(self.domain):
                for s in range(self.shots):
                    to_d = self.half * (s & 1) + self.chip_of(d, r)
                    to_s = (s & ~1) | (d & 1)
                    pairs.append((d * self.shots + s, to_d * self.shots + to_s))
            assert len({pair[1] for pair in pairs}) == count
            yield r, pairs


def swapped(value, axis, bit):
    count = lax.axis_size(axis)
    return lax.ppermute(value, axis, [(i, i ^ bit) for i in range(count)])


def tied(value, *others):
    return lax.optimization_barrier((value, *others))[0]


def swapped_round(value, axis, r):
    count = lax.axis_size(axis)
    return lax.ppermute(value, axis, [(i, (i + r) % count) for i in range(count)])


def gather_rows(lay, own_refs, other_refs, store):
    kc, c, unused, unused = lay.position()
    window = pl.ds(pl.multiple_of(lay.shift(c), TILE), lay.span)
    for core, refs in ((c, own_refs), (1 - c, other_refs)):
        for r, ref in enumerate(refs):
            source = 2 * lax.rem(kc - r + lay.half, lay.half) + core
            for part in range(lay.rows):
                store(source * lay.rows + part, ref.at[:, part, window, :])


def table_kernel(traces, wavelet, rec_x, rec_y, src_x, src_y, anchor, table):
    steps = traces.shape[1]
    table[...] = jnp.zeros_like(table)
    table[:steps] = traces[0]
    table[steps : steps + 1, :steps] = wavelet[...]
    row = (1, table.shape[1])
    table[steps + 1 : steps + 2] = rec_x[...].astype(jnp.float32)
    table[steps + 2 : steps + 3] = rec_y[...].astype(jnp.float32)
    for i, scalar in enumerate((src_x, src_y, anchor)):
        table[steps + 3 + i : steps + 4 + i] = jnp.full(row, scalar[0], jnp.int32).astype(jnp.float32)


def table_of(*arrays):
    steps, receivers = arrays[0].shape[1:]
    smem, vmem = (pl.BlockSpec(memory_space=space) for space in (pltpu.SMEM, pltpu.VMEM))
    return pl.pallas_call(
        table_kernel,
        out_shape=jax.ShapeDtypeStruct((-(-(steps + 6) // TILE) * TILE, receivers), jnp.float32),
        in_specs=[vmem] * 4 + [smem] * 3,
        out_specs=vmem,
        compiler_params=pltpu.CompilerParams(vmem_limit_bytes=2**21),
    )(*arrays)


def pulse_kernel(lay, mine, twin, receiver_out, source_out, scalars, padded):
    kc, c, d, works_on = lay.position()
    steps, lanes = lay.steps, receiver_out.shape[-1]
    window = lay.start(kc) + lay.shift(c) - lay.pad[0]
    table = jnp.where(works_on == c, mine[...], twin[...])

    def scalar(values, row):
        return jnp.max(values[row : row + 1]).astype(jnp.int32)

    src_x, src_y = scalar(table, steps + 3), scalar(table, steps + 4) - window
    first = jnp.clip(src_y, 0, lay.span - 1) & ~(TILE - 1)
    anchors = scalar(mine[...], steps + 5), scalar(twin[...], steps + 5)
    scalars[0], scalars[1] = src_x, first
    scalars[2] = jnp.where(c == 0, anchors[0], anchors[1])
    scalars[3] = jnp.where(c == 0, anchors[1], anchors[0])

    lane = lax.broadcasted_iota(jnp.int32, (TILE, lanes), 1)
    line = lax.broadcasted_iota(jnp.int32, (TILE, lanes), 0)
    spot = (lane == SRC_Z) & (line + first == src_y)
    at_step = lax.broadcasted_iota(jnp.int32, (1, table.shape[1]), 1)
    for step in range(steps):
        amount = jnp.sum(jnp.where(at_step == step, table[steps : steps + 1], 0.0))
        source_out[step] = jnp.where(spot, amount, 0.0)

    lines = lax.broadcasted_iota(jnp.int32, (lay.span, table.shape[1]), 0) + window
    there = (lines == table[steps + 2 : steps + 3].astype(jnp.int32)).astype(jnp.float32)
    padded[...] = jnp.zeros_like(padded)

    def one_row(row, unused):
        here = table[steps + 1 : steps + 2].astype(jnp.int32) == row
        padded[:steps] = jnp.where(here, table[:steps], 0.0)
        receiver_out[row] = lax.dot_general(
            there,
            padded[...],
            (((1,), (1,)), ((), ())),
            precision=lax.Precision.HIGHEST,
            preferred_element_type=jnp.float32,
        )
        return unused

    lax.fori_loop(0, lay.width, one_row, 0)


def pulses(lay, mine, twin, z_count):
    shapes = [(lay.width, lay.span, z_count), (lay.steps, TILE, z_count)]
    held = 4 * (2 * math.prod(shapes[0]) + z_count * mine.shape[1])
    smem, vmem = (pl.BlockSpec(memory_space=space) for space in (pltpu.SMEM, pltpu.VMEM))
    return pl.pallas_call(
        functools.partial(pulse_kernel, lay),
        out_shape=[jax.ShapeDtypeStruct(shape, jnp.float32) for shape in shapes]
        + [jax.ShapeDtypeStruct((4,), jnp.int32)],
        in_specs=[vmem] * 2,
        out_specs=[vmem, vmem, smem],
        scratch_shapes=[pltpu.VMEM((z_count, mine.shape[1]), jnp.float32)],
        compiler_params=pltpu.CompilerParams(vmem_limit_bytes=held + 2**21),
    )(mine, twin)


def sin_cos(angle):
    square = angle * angle
    sine, cosine = 1.0 / 6227020800.0, -1.0 / 87178291200.0
    for n in (11, 9, 7, 5, 3, 1):
        sine = sine * square + (-1.0) ** (n // 2) / math.factorial(n)
    for n in (12, 10, 8, 6, 4, 2, 0):
        cosine = cosine * square + (-1.0) ** (n // 2) / math.factorial(n)
    return sine * angle, cosine


def medium_kernel(velocity, eps, delta, tilt, azimuth, out):
    speed = velocity[...]
    out[0] = speed
    out[1] = speed * (1.0 + 2.0 * eps[...])
    out[2] = speed * jnp.sqrt(1.0 + 2.0 * delta[...])
    sin_tilt, unused = sin_cos(tilt[...])
    sine, cosine = sin_cos(0.5 * azimuth[...])
    out[3] = sin_tilt * (1.0 - 2.0 * sine * sine)
    out[4] = sin_tilt * (2.0 * sine * cosine)


def medium(*arrays):
    vmem = pl.BlockSpec(memory_space=pltpu.VMEM)
    return pl.pallas_call(
        medium_kernel,
        out_shape=jax.ShapeDtypeStruct((len(arrays),) + arrays[0].shape, jnp.float32),
        in_specs=[vmem] * len(arrays),
        out_specs=vmem,
    )(*arrays)


def make_coefs(raw_ref, coef_ref, lay):
    lane = lax.broadcasted_iota(jnp.int32, (TILE, raw_ref.shape[-1]), 1)
    last = raw_ref.shape[-1] - 1

    def from_below(value):
        return jnp.where(lane == 0, 0.0, pltpu.roll(value, 1, 1))

    def from_above(value):
        return jnp.where(lane == last, 0.0, pltpu.roll(value, last, 1))

    def one_row(row, unused):
        for tile in range(lay.span // TILE):
            lines = slice(TILE * tile, TILE * tile + TILE)
            n_x, n_y = raw_ref[0, row, lines, :], raw_ref[1, row, lines, :]
            xx, yy = n_x * n_x, n_y * n_y
            flat = xx + yy
            zz = 1.0 - flat
            half = 0.5 * jnp.sqrt(zz)
            xz, yz = half * n_x, half * n_y
            values = (
                xx, 1.0 - xx, yy, 1.0 - yy, 0.5 * n_x * n_y,
                from_below(zz), from_below(flat), from_below(xz), from_below(yz),
                from_above(zz), from_above(flat), from_above(xz), from_above(yz),
            )
            for i, value in enumerate(values):
                coef_ref[i, row, lines, :] = value
        return unused

    lax.fori_loop(0, lay.width, one_row, 0)


def run_steps(state, coef_ref, source, inject_ref, image_ref, lay):
    z_count = state.shape[-1]
    last = z_count - 1
    lane = lax.broadcasted_iota(jnp.int32, (TILE, z_count), 1)
    chunk = next(size for size in (8, 4, 2, 1) if lay.width % size == 0)

    def row_of(now, field, row, tile):
        base = TILE + TILE * tile
        middle = state[now, field, row, base : base + TILE, :]
        low = state[now, field, row, base - 1 : base - 1 + TILE, :]
        high = state[now, field, row, base + 1 : base + 1 + TILE, :]
        return middle, high - low, high + low

    def sweep(step, now, new, first, tile, wave):
        turn = lax.rem(REC_Z - step + z_count, z_count)
        lines = slice(TILE * tile, TILE * tile + TILE)
        inner = slice(TILE + TILE * tile, 2 * TILE + TILE * tile)
        pair = (2 * wave, 2 * wave + 1)
        before = [row_of(now, field, first, tile) for field in pair]
        here = [row_of(now, field, first + 1, tile) for field in pair]
        for i in range(chunk):
            row = first + i
            beyond = [row_of(now, field, row + 2, tile) for field in pair]
            coef = [coef_ref[n, row, lines, :] for n in range(COEFS)]
            xx, xx0, yy, yy0, xy = coef[:5]
            zz_b, zz0_b, xz_b, yz_b, zz_a, zz0_a, xz_a, yz_a = coef[5:13]
            velocity, axial_gain, cross_gain = coef[13:]

            def terms(field):
                f, diff_y, sum_y = here[field]
                sum_x = beyond[field][0] + before[field][0]
                diff_x = beyond[field][0] - before[field][0]
                mixed = beyond[field][1] - before[field][1]
                below = xz_b * diff_x + yz_b * diff_y
                above = xz_a * diff_x + yz_a * diff_y
                return f, sum_x, sum_y, xy * mixed, below, above

            p, sum_x, sum_y, mixed, below, above = terms(0)
            across = xx0 * sum_x + yy0 * sum_y - mixed
            across += pltpu.roll(zz0_b * p - below, last, 1) + pltpu.roll(zz0_a * p + above, 1, 1)
            twice_p = p + p
            across -= twice_p + twice_p
            q, sum_x, sum_y, mixed, below, above = terms(1)
            axial = xx * sum_x + yy * sum_y + mixed
            axial += pltpu.roll(zz_b * q + below, last, 1) + pltpu.roll(zz_a * q - above, 1, 1)
            twice_q = q + q
            axial -= twice_q
            old_p = state[new, pair[0], row + 1, inner, :]
            old_q = state[new, pair[1], row + 1, inner, :]
            new_p = (twice_p - old_p) + (axial_gain * across + cross_gain * axial)
            new_q = (twice_q - old_q) + (cross_gain * across + velocity * axial)
            if wave == 1:
                pulse = pltpu.roll(inject_ref[row, lines, :], turn, 1)
                pulse = velocity * jnp.where(lane == REC_Z, pulse, 0.0)
                new_p, new_q = new_p + pulse, new_q + pulse
            state[new, pair[0], row + 1, inner, :] = new_p
            state[new, pair[1], row + 1, inner, :] = new_q
            if wave == 1:
                image_ref[row, lines, :] += state[new, 0, row + 1, inner, :] * new_p
            before, here = here, beyond

    def one_step(step, now):
        def sweeps(wave):
            def one_chunk(first):
                for tile in range(lay.span // TILE):
                    sweep(step, now, 1 - now, first, tile, wave)

            if chunk == lay.width:
                one_chunk(0)
            else:
                lax.fori_loop(0, lay.width // chunk, lambda n, u: (one_chunk(n * chunk), u)[1], 0)

        sweeps(0)
        source_x, first, source_ref = source
        first = pl.multiple_of(first, TILE)
        pulse = coef_ref[COEFS - 3, source_x, pl.ds(first, TILE), :] * source_ref[step]
        for field in (0, 1):
            state[1 - now, field, source_x + 1, pl.ds(TILE + first, TILE), :] += pulse
        sweeps(1)

    def two_steps(i, unused):
        one_step(2 * i, 0)
        one_step(2 * i + 1, 1)
        return unused

    lax.fori_loop(0, lay.steps // 2, two_steps, 0)
    if lay.steps % 2:
        one_step(lay.steps - 1, 0)


def clear_edges(state, lay):
    rows, lines = state.shape[2], state.shape[3]
    edge = jnp.zeros((lines,) + state.shape[4:], jnp.float32)
    strip = jnp.zeros((rows, TILE) + state.shape[4:], jnp.float32)
    for time in range(state.shape[0]):
        for field in range(state.shape[1]):
            state[time, field, 0] = edge
            state[time, field, rows - 1] = edge
            state[time, field, :, :TILE] = strip
            state[time, field, :, lines - TILE :] = strip


def wave_kernel(lay, scalars, source_ref, receiver_ref, *refs):
    waves_own, waves_other, model_own, model_other = (refs[i * lay.half : (i + 1) * lay.half] for i in range(4))
    pieces, (raw, coef_ref, image_ref, state) = refs[4 * lay.half : -4], refs[-4:]
    clear_edges(state, lay)

    def store_wave(row, ref):
        for i in range(8):
            time, field = (i >> 1) & 1, 2 * (i >> 2) + (i & 1)
            state[time, field, row + 1, TILE : TILE + lay.span, :] = ref[i]

    def store_model(row, ref):
        for i in range(5):
            target = coef_ref.at[COEFS - 3 + i, row] if i < 3 else raw.at[i - 3, row]
            target[...] = ref[i]

    gather_rows(lay, waves_own, waves_other, store_wave)
    gather_rows(lay, model_own, model_other, store_model)
    make_coefs(raw, coef_ref, lay)
    image_ref[...] = jnp.zeros_like(image_ref)
    run_steps(state, coef_ref, (scalars[0], scalars[1], source_ref), receiver_ref, image_ref, lay)
    kc, c, d, unused = lay.position()
    skip = (2 * kc + c) * lay.own - (lay.start(kc) + lay.shift(c) - lay.pad[0])
    if lay.own % TILE == 0:
        skip = pl.multiple_of(skip, TILE)
    for r, piece in enumerate(pieces):
        first = lax.rem(d + r, lay.domain) * lay.rows
        for row in range(lay.rows):
            if lay.own % TILE == 0:
                piece[row] = image_ref[first + row, pl.ds(skip, lay.own), :]
            else:
                piece[row] = pltpu.roll(image_ref[first + row], lay.span - skip, 0)[: lay.own]


def frame_kernel(lay, scalars, owners, *refs, slab):
    pieces, outs, frame = refs[: lay.domain], refs[lay.domain : -1], refs[-1]
    unused, c, d, unused = lay.position()
    frame[...] = jnp.zeros_like(frame)
    room = -(-lay.own // TILE) * TILE + TILE
    filler = jnp.zeros((room - lay.own, frame.shape[-1]), jnp.float32)
    for r, piece in enumerate(pieces):
        source = lax.rem(d - r + lay.domain, lay.domain)
        place = scalars[2 + source // lay.half] + (2 * lax.rem(source, lay.half) + c) * lay.own
        first = pl.multiple_of(place & ~(TILE - 1), TILE)
        for row in range(lay.rows):
            moved = pltpu.roll(jnp.concatenate([piece[row], filler]), place & (TILE - 1), 0)
            frame[row, pl.ds(first, room), :] += moved
    for r, out in enumerate(outs):
        first = pl.multiple_of(owners[lax.axis_index("shot") ^ r] * slab, TILE)
        for row in range(lay.rows):
            out[row] = frame[row, pl.ds(first, slab), :]


def call(kernel, cost, lay, outs, scratch, scalars, *operands):
    smem = pl.BlockSpec(memory_space=pltpu.SMEM)
    vmem = pl.BlockSpec(memory_space=pltpu.VMEM)
    held = sum(4 * math.prod(array.shape) for array in [*operands, *outs, *scratch])
    return pl.pallas_call(
        functools.partial(kernel, lay),
        out_shape=outs,
        in_specs=[smem] * len(scalars) + [vmem] * len(operands),
        out_specs=[vmem] * len(outs),
        scratch_shapes=scratch,
        compiler_params=pltpu.CompilerParams(vmem_limit_bytes=held + held // 8 + 2**21),
        cost_estimate=pl.CostEstimate(flops=0, bytes_accessed=cost, transcendentals=0),
    )(*scalars, *operands)


def per_device(
    velocity,
    thomsen_eps,
    thomsen_delta,
    tilt_angle,
    azimuth,
    shot_anchor,
    source_x,
    source_y,
    wavelet,
    receiver_x,
    receiver_y,
    traces,
    source_now,
    source_before,
    receiver_now,
    receiver_before,
    slab_owner,
):
    rows, lines, z_count = source_now.shape[2:]
    steps = wavelet.shape[1]
    domain, shots = lax.axis_size("domain"), lax.axis_size("shot")
    lay = Layout(domain, shots, rows, lines, steps)
    d, s = lax.axis_index("domain"), lax.axis_index("shot")
    zero = jnp.int32(0)

    tight = lay.pad == (0, 0)

    def wave_messages(fields):
        fields = [jnp.pad(field[0], ((0, 0), (0, 0), lay.pad, (0, 0))) for field in fields]
        messages = []
        for r in range(lay.half):
            first = lay.start(lay.chip_of(d, r))
            messages.append(
                jnp.concatenate([lax.dynamic_slice_in_dim(field, first, lay.chip, 2) for field in fields])
            )
        return messages

    def send(messages):
        return [lax.ppermute(messages[r], ("domain", "shot"), pairs) for r, pairs in lay.rounds()]

    def other_core(messages):
        return [swapped(message, "shot", 1) for message in messages]

    messages = wave_messages((source_now, source_before, receiver_now, receiver_before))
    waves = send(messages)
    model = medium(velocity, thomsen_eps, thomsen_delta, tilt_angle, azimuth)
    slab = model.shape[2]
    whole = jnp.zeros(model.shape[:2] + (shots * slab, z_count), jnp.float32)
    for r in range(shots):
        block = swapped(model, "shot", r) if r else model
        whole = lax.dynamic_update_slice(whole, block, (zero, zero, (s ^ r) * slab, zero))
    model = whole
    anchor = shot_anchor[0]
    if tight:
        first_line = anchor
    else:
        model = lax.dynamic_slice_in_dim(model, anchor, lines, 2)
        model = jnp.pad(model, ((0, 0), (0, 0), lay.pad, (0, 0)))
        first_line = zero
    messages = []
    for r in range(lay.half):
        first = first_line + lay.start(lay.chip_of(d, r))
        messages.append(lax.dynamic_slice_in_dim(model, first, lay.chip, 2))
    models = send(messages)
    *waves, models[0] = lax.optimization_barrier((*waves, models[0]))
    waves_other = other_core(waves)

    traces, waves[0] = lax.optimization_barrier((traces, waves[0]))
    table = table_of(traces, wavelet, receiver_x, receiver_y, source_x, source_y, shot_anchor)
    receiver_pulse, source_pulse, scalars = pulses(lay, table, swapped(table, "shot", 1), z_count)
    *models, receiver_pulse = lax.optimization_barrier((*models, receiver_pulse))
    models_other = other_core(models)
    block = (lay.width, lay.span, z_count)
    pieces = call(
        wave_kernel,
        60_000_000,
        lay,
        [jax.ShapeDtypeStruct((rows, lay.own, z_count), jnp.float32)] * domain,
        [
            pltpu.VMEM((2,) + block, jnp.float32),
            pltpu.VMEM((COEFS,) + block, jnp.float32),
            pltpu.VMEM(block, jnp.float32),
            pltpu.VMEM((2, 4, lay.width + 2, lay.span + 2 * TILE, z_count), jnp.float32),
        ],
        (scalars,),
        source_pulse,
        receiver_pulse,
        *waves,
        *waves_other,
        *models,
        *models_other,
    )

    pieces = [
        swapped_round(piece, "domain", r) if r else piece for r, piece in enumerate(pieces)
    ]
    room = -(-lay.own // TILE) * TILE + TILE
    parts = call(
        functools.partial(frame_kernel, slab=slab),
        2_000_000,
        lay,
        [jax.ShapeDtypeStruct((rows, slab, z_count), jnp.float32)] * shots,
        [pltpu.VMEM((rows, shots * slab + room, z_count), jnp.float32)],
        (scalars, slab_owner),
        *pieces,
    )
    parts, bit = list(parts), 1
    while bit < shots:
        for r in range(0, shots, 2 * bit):
            parts[r] = parts[r] + swapped(parts[r + bit], "shot", bit)
        bit *= 2
    total = parts[0]
    return total / steps


def solution(mesh):
    in_specs = (
        P(("groups", "domain"), "shot", None),
        P(("groups", "domain"), "shot", None),
        P(("groups", "domain"), "shot", None),
        P(("groups", "domain"), "shot", None),
        P(("groups", "domain"), "shot", None),
        P(("groups", "shot")),
        P(("groups", "shot")),
        P(("groups", "shot")),
        P(("groups", "shot"), None),
        P(("groups", "shot"), None),
        P(("groups", "shot"), None),
        P(("groups", "shot"), None, None),
        P(("groups", "shot"), None, "domain", None, None),
        P(("groups", "shot"), None, "domain", None, None),
        P(("groups", "shot"), None, "domain", None, None),
        P(("groups", "shot"), None, "domain", None, None),
        P("groups"),
    )
    out_specs = P(("groups", "domain"), "shot", None)
    return jax.shard_map(
        per_device, mesh=mesh, in_specs=in_specs, out_specs=out_specs, check_vma=False
    )
```
